256 devices in a mesh: blk: 128 (over y_hi, x, z, core), fsdp: 2 (over y_lo).
Axes of the slice: x: 4, y: 4 (y_hi: 2, y_lo: 2; y = y_hi * 2 + y_lo), z: 8, core: 2. Of those that a mesh axis runs over, the one named last changes fastest.
Arguments:
- image_features: bfloat16 [65536, 1152], P(('blk', 'fsdp')), may hold values from -6 to 6
- text_features: bfloat16 [65536, 1152], P(('blk', 'fsdp')), may hold values from -6 to 6
- image_head: bfloat16 [1152, 1152], P('fsdp'), may hold values from -0.1875 to 0.1875
- text_head: bfloat16 [1152, 1152], P('fsdp'), may hold values from -0.1875 to 0.1875
- pair_index: int32 [256, 256], P(('blk', 'fsdp')), may hold values from 0 to 255, each once within a row
- logit_scale: float32 [1], replicated, may hold values from 2 to 8
- logit_bias: float32 [1], replicated, may hold values from -1 to 0
Outputs:
- image_head_grad: float32 [1152, 1152], P('fsdp')
- text_head_grad: float32 [1152, 1152], P('fsdp')
The draws below stay inside these ranges and needn't reach their ends.
Inputs may be any that keep to these rules, and one draw needn't show every extreme that they name: Each row of pair_index names every row 0 to 255 of its block exactly once.
All inputs are finite; a program needn't handle non-finite values.
Results may differ from the reference program's by a relative error of at most 0.004.
Values may be sent and summed in bfloat16 or wider, within the bound.
A program may use at most 128 MiB of HBM per device.

```python
import math
import jax
import jax.numpy as jnp
from jax import lax

E = 1152
ROWS = 256
STEPS = 8
BLOCKS = 256
BATCH = 65536


def shard_levels(key, dims, split, smallest, high):
    gain, own = 1.0, jax.random.fold_in(key, 6)
    for axis_at, shards_of in split:
        steps = jnp.exp(jax.random.uniform(jax.random.fold_in(own, axis_at), (shards_of,), jnp.float32, smallest / len(split), high / len(split)))
        gain = gain * jnp.repeat(steps, dims[axis_at] // shards_of).reshape([-1 if axis == axis_at else 1 for axis in range(len(dims))])
    return gain


def bell_draw(stream_key, extent, spread, reach, shards=(), kind=jnp.bfloat16):
    values = spread * jax.random.normal(stream_key, extent, jnp.float32)
    if shards:
        values = values * shard_levels(stream_key, extent, shards, -0.22, 0.18)
    return jnp.clip(values, -reach, reach).astype(kind)


def setup_inputs(seed: int = 0) -> dict:
    keys = jax.random.split(jax.random.key(seed), 8)
    return {
        "image_features": bell_draw(keys[0], (BATCH, E), 1.0, 6.0, ((0, 256),)),
        "text_features": bell_draw(keys[1], (BATCH, E), 1.0, 6.0, ((0, 256),)),
        "image_head": bell_draw(keys[2], (E, E), E ** -0.5, 0.1875, ((0, 2),)),
        "text_head": bell_draw(keys[3], (E, E), E ** -0.5, 0.1875, ((0, 2),)),
        "pair_index": jax.vmap(lambda own: jax.random.permutation(own, ROWS))(jax.random.split(keys[4], BLOCKS)).reshape((BLOCKS, ROWS)).astype(jnp.int32),
        "logit_scale": jnp.clip(jnp.exp(jax.random.uniform(keys[5], (1,), jnp.float32, math.log(2.0), math.log(8.0))), 2.0, 8.0),
        "logit_bias": jnp.clip(jax.random.uniform(keys[6], (1,), jnp.float32, -1.0, 0.0), -1.0, 0.0),
    }


def unit_rows(features, head):
    raw = jnp.dot(features, head, preferred_element_type=jnp.float32)
    inverse = lax.rsqrt(lax.optimization_barrier(jnp.sum(raw * raw, axis=1, keepdims=True)) + 1e-06)
    return (raw * inverse, inverse)

def raw_grad(unit, inverse, emb_grad):
    inner = lax.optimization_barrier(jnp.sum(unit * emb_grad, axis=1, keepdims=True))
    return ((emb_grad - unit * inner) * inverse).astype(jnp.bfloat16)

def reference(image_features, text_features, image_head, text_head, pair_index, logit_scale, logit_bias):
    scale = logit_scale[0]
    bias = logit_bias[0]
    image_unit, image_inverse = unit_rows(image_features, image_head)
    text_unit, text_inverse = unit_rows(text_features, text_head)
    image_emb = image_unit.astype(jnp.bfloat16).astype(jnp.float32).reshape(BLOCKS, ROWS, E)
    text_emb = text_unit.astype(jnp.bfloat16).astype(jnp.float32).reshape(BLOCKS, ROWS, E)
    positive = jnp.arange(ROWS, dtype=jnp.int32)[None, None, :] == pair_index[:, :, None]
    image_emb_grad = jnp.zeros((BLOCKS, ROWS, E), jnp.float32)
    text_emb_grad = jnp.zeros((BLOCKS, ROWS, E), jnp.float32)
    for step in range(STEPS):
        text_block = jnp.roll(text_emb, step, axis=0)
        scores = scale * jnp.einsum('qre,qse->qrs', image_emb, text_block) + bias
        if step == 0:
            label = jnp.where(positive, 1.0, -1.0).astype(jnp.float32)
        else:
            label = -jnp.ones_like(scores)
        grad = (-(1.0 / STEPS) * label * jax.nn.sigmoid(-label * scores)).astype(jnp.bfloat16).astype(jnp.float32)
        image_emb_grad = image_emb_grad + scale * jnp.einsum('qrs,qse->qre', grad, text_block)
        term = scale * jnp.einsum('qrs,qre->qse', grad, image_emb)
        text_emb_grad = text_emb_grad + jnp.roll(term, -step, axis=0)
    image_raw_grad = raw_grad(image_unit, image_inverse, image_emb_grad.reshape(BATCH, E))
    text_raw_grad = raw_grad(text_unit, text_inverse, text_emb_grad.reshape(BATCH, E))
    image_head_grad = jnp.dot(image_features.T, image_raw_grad, preferred_element_type=jnp.float32)
    text_head_grad = jnp.dot(text_features.T, text_raw_grad, preferred_element_type=jnp.float32)
    return (image_head_grad, text_head_grad)
```

```python
import jax
import jax.numpy as jnp
from jax import lax
from jax.experimental import pallas as pl
from jax.experimental.pallas import tpu as pltpu
from jax.sharding import PartitionSpec as P

STEPS = 8
MESH = pl.DeviceIdType.MESH
ROWS = 256
E = 1152
HALF = E // 2
SLOTS = 5
PARTS = 3
WIDE = E // PARTS
NEAR = 160
XROWS = HALF // 4
PIECE = 16
PWIDE = WIDE + 128


def device_of(x, yh, f, z, core):
    return (((yh * 4 + x) * 8 + z) * 2 + core, f)


def shifted(index, by):
    other = lax.rem(index + (by + 256), 256)
    return (lax.div(other, 2), lax.rem(other, 2))


def is_equal(n, k):
    gap = n - k
    return 1 - lax.div(gap * gap + 99, 100)


def kernel(
    image_ref,
    text_ref,
    image_head_ref,
    text_head_ref,
    pair_ref,
    scale_ref,
    bias_ref,
    image_out,
    text_out,
    feats,
    feats_t,
    head,
    raw,
    inv,
    emb,
    emb_other,
    grad,
    raw_grad,
    pairs,
    signs,
    y_out,
    y_in,
    total,
    x_out,
    x_in,
    x_sum,
    z_out,
    z_in,
    z_sum,
    y2_in,
    final,
    z_all,
    mine,
    other,
    feat_send,
    feat_recv,
    head_send,
    head_recv,
    pair_send,
    pair_recv,
    emb_send,
    emb_recv,
    y_send,
    y_recv,
    x_send,
    x_recv,
    z_send,
    z_recv,
    y2_send,
    y2_recv,
    zag_send,
    zag_recv,
    xag_send,
    xag_recv,
    core_send,
    core_recv,
    out_sem,
):
    blk = lax.axis_index("blk")
    f = lax.axis_index("fsdp")
    core = lax.rem(blk, 2)
    z = lax.rem(lax.div(blk, 2), 8)
    x = lax.rem(lax.div(blk, 16), 4)
    yh = lax.div(blk, 64)
    index = blk * 2 + f
    sibling = device_of(x, yh, f, z, 1 - core)
    near = device_of(x, yh, 1 - f, z, core)
    far = device_of(x, 1 - yh, 1 - f, z, core)
    across = device_of(x, 1 - yh, f, z, core)
    x_peers = [device_of(lax.rem(x + k, 4), yh, f, z, core) for k in range(1, 4)]
    z_peers = [device_of(x, yh, f, lax.rem(z + k, 8), core) for k in range(1, 8)]
    step = 3 - 2 * lax.rem(core + f, 2)

    barrier = pltpu.get_barrier_semaphore()

    def hello(device):
        pl.semaphore_signal(barrier, inc=1, device_id=device, device_id_type=MESH)

    for device in [sibling, near, far, across] + x_peers + z_peers:
        hello(device)

    @pl.when(core == 0)
    def _():
        hello(shifted(index, 1))
        hello(shifted(index, 3))

    @pl.when(core == 1)
    def _():
        hello(shifted(index, -4))
        hello(shifted(index, -6))

    def rows_of(ref, slot):
        start = slot * ROWS
        if not isinstance(slot, int):
            start = pl.multiple_of(start, ROWS)
        return ref.at[pl.ds(start, ROWS)]

    def remote(src, dst, send, recv, device):
        return pltpu.make_async_remote_copy(
            src_ref=src, dst_ref=dst, send_sem=send, recv_sem=recv,
            device_id=device, device_id_type=MESH,
        )

    def feat_copy(src, slot, which, device):
        return remote(src, rows_of(feats, slot), feat_send.at[which], feat_recv.at[slot], device)

    own_half = pl.multiple_of(f * HALF, 16)
    own_pair = pltpu.make_async_copy(pair_ref, pairs.at[0], pair_send.at[0])
    own_pair.start()

    @pl.when(core == 0)
    def _():
        pltpu.make_async_copy(image_ref, rows_of(feats, 0), feat_recv.at[0]).start()
        pltpu.make_async_copy(image_head_ref, head.at[pl.ds(own_half, HALF)], head_recv.at[0]).start()

    @pl.when(core == 1)
    def _():
        pltpu.make_async_copy(text_ref, rows_of(feats, 0), feat_recv.at[0]).start()
        pltpu.make_async_copy(text_head_ref, head.at[pl.ds(own_half, HALF)], head_recv.at[0]).start()

    pl.semaphore_wait(barrier, 16)

    def head_copies(src):
        first = pl.multiple_of(f * HALF, 16)
        second = pl.multiple_of(f * HALF + NEAR, 16)
        return (
            remote(src.at[pl.ds(0, NEAR)], head.at[pl.ds(first, NEAR)],
                   head_send.at[0], head_recv.at[1], near),
            remote(src.at[pl.ds(NEAR, HALF - NEAR)], head.at[pl.ds(second, HALF - NEAR)],
                   head_send.at[1], head_recv.at[2], far),
        )

    pair_copy = remote(pair_ref, pairs.at[1], pair_send.at[1], pair_recv, sibling)

    @pl.when(core == 0)
    def _():
        for copy in head_copies(image_head_ref):
            copy.start()
        feat_copy(image_ref, step, 0, shifted(index, -step)).start()
        feat_copy(text_ref, 1, 1, sibling).start()
        feat_copy(text_ref, 3, 2, shifted(index, 6)).start()

    @pl.when(core == 1)
    def _():
        for copy in head_copies(text_head_ref):
            copy.start()
        feat_copy(image_ref, step, 0, shifted(index, -step)).start()
        feat_copy(image_ref, 2, 1, sibling).start()
        feat_copy(text_ref, 2, 2, shifted(index, 4)).start()

    pair_copy.start()

    grad[...] = jnp.zeros_like(grad)

    @pl.when(core == 0)
    def _():
        rows_of(feats, 4)[...] = jnp.zeros((ROWS, E), jnp.bfloat16)
        rows_of(raw_grad, 4)[...] = jnp.zeros((ROWS, E), jnp.bfloat16)

    own_pair.wait()
    pair_copy.wait()
    signs[2] = jnp.ones((ROWS, ROWS), jnp.float32)
    for which in range(2):
        hit = lax.broadcasted_iota(jnp.int32, (ROWS, ROWS), 0) == pairs[which]
        sign = jnp.where(hit, -1.0, 1.0).astype(jnp.float32)

        @pl.when(core == 0)
        def _():
            signs[which] = sign.T

        @pl.when(core == 1)
        def _():
            signs[1 - which] = sign

    def feat_wait(slot):
        pltpu.make_async_copy(rows_of(feats, slot), rows_of(feats, slot), feat_recv.at[slot]).wait()

    def turn(slot):
        feats_t[:, slot * ROWS : (slot + 1) * ROWS] = rows_of(feats, slot)[...].T

    forward = feat_copy(rows_of(feats, 2), 4, 3, shifted(index, 4))
    for slot in (0, 1, 2, 3):
        feat_wait(slot)
        if slot == 2:
            @pl.when(core == 1)
            def _():
                forward.start()
        turn(slot)

    other_half = pl.multiple_of((1 - f) * HALF, 16)
    other_rest = pl.multiple_of((1 - f) * HALF + NEAR, 16)

    def head_wait(rows, sem):
        pltpu.make_async_copy(head.at[rows], head.at[rows], head_recv.at[sem]).wait()

    head_wait(pl.ds(own_half, HALF), 0)
    head_wait(pl.ds(other_half, NEAR), 1)
    head_wait(pl.ds(other_rest, HALF - NEAR), 2)

    def emb_copy(slot):
        return remote(rows_of(emb, slot), rows_of(emb_other, slot),
                      emb_send.at[slot], emb_recv.at[slot], sibling)

    def embed(slot):
        product = jnp.dot(rows_of(feats, slot)[...], head[...], preferred_element_type=jnp.float32)
        inverse = lax.rsqrt(jnp.sum(product * product, axis=1, keepdims=True) + 1e-06)
        unit = product * inverse
        rows_of(raw, slot)[...] = unit
        rows_of(inv, slot)[...] = inverse
        rows_of(emb, slot)[...] = unit.astype(jnp.bfloat16)
        emb_copy(slot).start()

    def embed_step(slot, carry):
        embed(slot)
        return carry

    lax.fori_loop(0, 4, embed_step, 0)

    @pl.when(core == 1)
    def _():
        feat_wait(4)
        embed(4)

    turn(4)

    for slot in range(4):
        @pl.when(core == 0)
        def _():
            emb_copy(slot).wait_recv()

        @pl.when(core == 1)
        def _():
            emb_copy(slot).wait_recv()

    @pl.when(core == 0)
    def _():
        emb_copy(4).wait_recv()

    scale = scale_ref[0]
    bias = bias_ref[0]

    def item(n, carry):
        at0 = lax.div(n, 2)
        at1 = lax.div(n + 1, 2)
        col0 = 1 - lax.div(at0, 2) + 2 * lax.rem(n, 2)
        col1 = 2 * lax.rem(n + 1, 2)
        at = at0 + core * (at1 - at0)
        col = col0 + core * (col1 - col0)
        kind = 2 - (
            is_equal(n, 0) * (2 - core) + is_equal(n, 4) * (1 - core) + is_equal(n, 1) * 2 * core
        )
        block = emb_other[pl.ds(pl.multiple_of(col * ROWS, ROWS), 2 * ROWS)]
        scores = scale * lax.dot_general(
            rows_of(emb, at)[...], block, (((1,), (1,)), ((), ())),
            preferred_element_type=jnp.float32,
        ) + bias
        sign = signs[kind]
        first = sign * (0.0625 + 0.0625 * jnp.tanh((0.5 * sign) * scores[:, :ROWS]))
        second = 0.0625 + 0.0625 * jnp.tanh(0.5 * scores[:, ROWS:])
        slope = jnp.concatenate([first, second], axis=1).astype(jnp.bfloat16)
        here = rows_of(grad, at)
        here[...] += jnp.dot(slope, block, preferred_element_type=jnp.float32)
        return carry

    lax.fori_loop(0, 8, item, 0)

    def finish(slot, carry):
        unit = rows_of(raw, slot)[...]
        slope = scale * rows_of(grad, slot)[...]
        inner = jnp.sum(unit * slope, axis=1, keepdims=True)
        rows_of(raw_grad, slot)[...] = (
            (slope - unit * inner) * rows_of(inv, slot)[...]
        ).astype(jnp.bfloat16)
        return carry

    lax.fori_loop(0, 4, finish, 0)

    @pl.when(core == 1)
    def _():
        finish(4, 0)

    SIDE = HALF // 2

    def y_copies(j):
        return (
            remote(y_out.at[j, pl.ds(0, SIDE)], y_in.at[j, pl.ds(0, SIDE)],
                   y_send.at[j, 0], y_recv.at[j, 0], near),
            remote(y_out.at[j, pl.ds(SIDE, SIDE)], y_in.at[j, pl.ds(SIDE, SIDE)],
                   y_send.at[j, 1], y_recv.at[j, 1], far),
        )

    for j in range(PARTS):
        cols = pl.ds(j * WIDE, WIDE)
        y_out[j] = jnp.dot(
            feats_t[pl.ds(other_half, HALF), :], raw_grad[:, cols], preferred_element_type=jnp.float32
        ).astype(jnp.bfloat16)
        for copy in y_copies(j):
            copy.start()
    for j in range(PARTS):
        cols = pl.ds(j * WIDE, WIDE)
        total[j] = jnp.dot(
            feats_t[pl.ds(own_half, HALF), :], raw_grad[:, cols], preferred_element_type=jnp.float32
        )

    def x_copy(j, k):
        return remote(x_out.at[j, k - 1], x_in.at[j, k - 1],
                      x_send.at[j, k - 1], x_recv.at[j, k - 1], x_peers[k - 1])

    def z_copy(j, k):
        return remote(z_out.at[j, k - 1], z_in.at[j, k - 1],
                      z_send.at[j, k - 1], z_recv.at[j, k - 1], z_peers[k - 1])

    def y2_copy(j):
        return remote(z_sum.at[j], y2_in.at[j], y2_send.at[j], y2_recv.at[j], across)

    def zag_copy(j, k):
        return remote(final.at[j], z_all.at[j, k - 1],
                      zag_send.at[j, k - 1], zag_recv.at[j, k - 1], z_peers[k - 1])

    x_rows = pl.ds(pl.multiple_of(x * XROWS, 16), XROWS)

    def xag_copy(j, k):
        return remote(mine.at[j, x_rows], mine.at[j, x_rows],
                      xag_send.at[j, k - 1], xag_recv.at[j, k - 1], x_peers[k - 1])

    def core_copy(j):
        return remote(mine.at[j], other.at[j], core_send.at[j], core_recv.at[j], sibling)

    def stage_a(j):
        for copy in y_copies(j):
            copy.wait_recv()
        for k in range(1, 4):
            rows = pl.ds(pl.multiple_of(lax.rem(x + k, 4) * XROWS, 16), XROWS)
            x_out[j, k - 1] = (total[j, rows] + y_in[j, rows].astype(jnp.float32)).astype(jnp.bfloat16)
            x_copy(j, k).start()
        x_sum[j] = total[j, x_rows] + y_in[j, x_rows].astype(jnp.float32)

    def extra_cols(at):
        return pl.ds(pl.multiple_of(lax.div(at * 3, 8) * 128, 128), 128)

    def stage_b(j):
        for k in range(1, 4):
            x_copy(j, k).wait_recv()
        x_sum[j] = (
            x_sum[j] + x_in[j, 0].astype(jnp.float32)
        ) + (x_in[j, 1].astype(jnp.float32) + x_in[j, 2].astype(jnp.float32))
        for k in range(1, 8):
            at = lax.rem(z + k, 8)
            rows = pl.ds(pl.multiple_of(at * PIECE, PIECE), PIECE)
            z_out[j, k - 1, :, :WIDE] = x_sum[j, rows].astype(jnp.bfloat16)
            z_out[j, k - 1, :, WIDE:] = x_sum[j, 8 * PIECE :, extra_cols(at)].astype(jnp.bfloat16)
            z_copy(j, k).start()
        z_sum[j, :, :WIDE] = x_sum[j, pl.ds(pl.multiple_of(z * PIECE, PIECE), PIECE)]
        z_sum[j, :, WIDE:] = x_sum[j, 8 * PIECE :, extra_cols(z)]

    def stage_c(j):
        for k in range(1, 8):
            z_copy(j, k).wait_recv()
        acc = z_sum[j]
        for k in range(1, 8):
            acc = acc + z_in[j, k - 1].astype(jnp.float32)
        z_sum[j] = acc
        y2_copy(j).start()

    def place(j, at, piece):
        rows = pl.ds(pl.multiple_of(x * XROWS + at * PIECE, PIECE), PIECE)
        mine[j, rows] = piece[:, :WIDE]
        last = pl.ds(pl.multiple_of(x * XROWS + 8 * PIECE, PIECE), PIECE)
        for n, source in enumerate((0, 3, 6)):
            @pl.when(at == source)
            def _():
                mine[j, last, n * 128 : (n + 1) * 128] = piece[:, WIDE:]

    def stage_d(j):
        y2_copy(j).wait_recv()
        final[j] = (z_sum[j] + y2_in[j]).astype(jnp.bfloat16)
        for k in range(1, 8):
            zag_copy(j, k).start()
        place(j, z, final[j])

    def stage_e(j):
        for k in range(1, 8):
            zag_copy(j, k).wait_recv()
            place(j, lax.rem(z + 8 - k, 8), z_all[j, k - 1])
        for k in range(1, 4):
            xag_copy(j, k).start()

    def stage_f(j):
        for k in range(1, 4):
            rows = pl.ds(pl.multiple_of(lax.rem(x + 4 - k, 4) * XROWS, 16), XROWS)
            remote(mine.at[j, rows], mine.at[j, rows],
                   xag_send.at[j, k - 1], xag_recv.at[j, k - 1], x_peers[k - 1]).wait_recv()
        core_copy(j).start()

    def out_copies(j, first, second):
        cols = pl.ds(j * WIDE, WIDE)
        return (
            pltpu.make_async_copy(mine.at[j], first.at[:, cols], out_sem.at[j, 0]),
            pltpu.make_async_copy(other.at[j], second.at[:, cols], out_sem.at[j, 1]),
        )

    def stage_g(j):
        core_copy(j).wait_recv()

        @pl.when(core == 0)
        def _():
            for copy in out_copies(j, image_out, text_out):
                copy.start()

        @pl.when(core == 1)
        def _():
            for copy in out_copies(j, text_out, image_out):
                copy.start()

    stages = (stage_a, stage_b, stage_c, stage_d, stage_e, stage_f, stage_g)
    for turn_at in range(len(stages) + PARTS - 1):
        for j in range(PARTS):
            if 0 <= turn_at - j < len(stages):
                stages[turn_at - j](j)

    for copy in head_copies(image_head_ref):
        copy.wait_send()
    for which in range(3):
        feat_copy(image_ref, 0, which, sibling).wait_send()

    @pl.when(core == 1)
    def _():
        forward.wait_send()
        emb_copy(4).wait_send()

    for slot in range(4):
        emb_copy(slot).wait_send()
    for j in range(PARTS):
        for copy in y_copies(j):
            copy.wait_send()
        for k in range(1, 4):
            x_copy(j, k).wait_send()
            xag_copy(j, k).wait_send()
        for k in range(1, 8):
            z_copy(j, k).wait_send()
            zag_copy(j, k).wait_send()
        y2_copy(j).wait_send()
        core_copy(j).wait_send()
        for copy in out_copies(j, image_out, text_out):
            copy.wait()


def on_device(
    image_features, text_features, image_head, text_head, pair_index, logit_scale, logit_bias
):
    hbm = pl.BlockSpec(memory_space=pl.ANY)
    smem = pl.BlockSpec(memory_space=pltpu.SMEM)
    bf16, f32 = jnp.bfloat16, jnp.float32
    vmem = pltpu.VMEM
    dma = pltpu.SemaphoreType.DMA
    image_half, text_half = pl.pallas_call(
        kernel,
        out_shape=(
            jax.ShapeDtypeStruct((HALF, E), bf16),
            jax.ShapeDtypeStruct((HALF, E), bf16),
        ),
        in_specs=[hbm, hbm, hbm, hbm, hbm, smem, smem],
        out_specs=(hbm, hbm),
        scratch_shapes=[
            vmem((SLOTS * ROWS, E), bf16),
            vmem((E, SLOTS * ROWS), bf16),
            vmem((E, E), bf16),
            vmem((SLOTS * ROWS, E), f32),
            vmem((SLOTS * ROWS, 1), f32),
            vmem((SLOTS * ROWS, E), bf16),
            vmem((SLOTS * ROWS, E), bf16),
            vmem((SLOTS * ROWS, E), f32),
            vmem((SLOTS * ROWS, E), bf16),
            vmem((2, 1, ROWS), jnp.int32),
            vmem((3, ROWS, ROWS), f32),
            vmem((PARTS, HALF, WIDE), bf16),
            vmem((PARTS, HALF, WIDE), bf16),
            vmem((PARTS, HALF, WIDE), f32),
            vmem((PARTS, 3, XROWS, WIDE), bf16),
            vmem((PARTS, 3, XROWS, WIDE), bf16),
            vmem((PARTS, XROWS, WIDE), f32),
            vmem((PARTS, 7, PIECE, PWIDE), bf16),
            vmem((PARTS, 7, PIECE, PWIDE), bf16),
            vmem((PARTS, PIECE, PWIDE), f32),
            vmem((PARTS, PIECE, PWIDE), f32),
            vmem((PARTS, PIECE, PWIDE), bf16),
            vmem((PARTS, 7, PIECE, PWIDE), bf16),
            vmem((PARTS, HALF, WIDE), bf16),
            vmem((PARTS, HALF, WIDE), bf16),
            dma((4,)),
            dma((SLOTS,)),
            dma((2,)),
            dma((3,)),
            dma((2,)),
            dma,
            dma((SLOTS,)),
            dma((SLOTS,)),
            dma((PARTS, 2)),
            dma((PARTS, 2)),
            dma((PARTS, 3)),
            dma((PARTS, 3)),
            dma((PARTS, 7)),
            dma((PARTS, 7)),
            dma((PARTS,)),
            dma((PARTS,)),
            dma((PARTS, 7)),
            dma((PARTS, 7)),
            dma((PARTS, 3)),
            dma((PARTS, 3)),
            dma((PARTS,)),
            dma((PARTS,)),
            dma((PARTS, 2)),
        ],
        compiler_params=pltpu.CompilerParams(
            collective_id=0, has_side_effects=True, vmem_limit_bytes=60 * 2**20
        ),
        cost_estimate=pl.CostEstimate(
            flops=12 * 10**9, bytes_accessed=12 * 10**6, transcendentals=10**6
        ),
    )(image_features, text_features, image_head, text_head, pair_index, logit_scale, logit_bias)
    return (image_half.astype(f32), text_half.astype(f32))


def solution(mesh):
    placed = (
        P(("blk", "fsdp"), None),
        P(("blk", "fsdp"), None),
        P("fsdp", None),
        P("fsdp", None),
        P(("blk", "fsdp"), None),
        P(),
        P(),
    )
    return jax.shard_map(
        on_device,
        mesh=mesh,
        in_specs=placed,
        out_specs=(P("fsdp", None), P("fsdp", None)),
        check_vma=False,
    )
```

```python
import jax
import jax.numpy as jnp
from jax import lax
from jax.experimental import pallas as pl
from jax.experimental.pallas import tpu as pltpu
from jax.sharding import PartitionSpec as P

STEPS = 8
MESH = pl.DeviceIdType.MESH
ROWS = 256
E = 1152
HALF = E // 2
SLOTS = 5
WIDTHS = (384, 384, 384)
PARTS = len(WIDTHS)
STARTS = tuple(sum(WIDTHS[:n]) for n in range(PARTS))
BITS = 4
RELAY = 0
BIT = ROWS // BITS
DIRECT = 256
SHARE = (HALF - DIRECT) // 4
SHARE_FAR = 48
SHARE_NEAR = SHARE - SHARE_FAR
XROWS = HALF // 4
PIECE = 16
PWIDE = E + 128 * PARTS


def device_of(x, yh, f, z, core):
    return (((yh * 4 + x) * 8 + z) * 2 + core, f)


def shifted(index, by):
    other = lax.rem(index + (by + 256), 256)
    return (lax.div(other, 2), lax.rem(other, 2))


def is_equal(n, k):
    gap = n - k
    return 1 - lax.div(gap * gap + 99, 100)


def kernel(
    image_ref,
    text_ref,
    image_head_ref,
    text_head_ref,
    pair_ref,
    scale_ref,
    bias_ref,
    image_out,
    text_out,
    feats,
    feats_t,
    head,
    raw,
    inv,
    emb,
    emb_other,
    grad,
    raw_grad,
    relay,
    pairs,
    signs,
    y_out,
    y_in,
    total,
    x_out,
    x_in,
    x_sum,
    z_out,
    z_in,
    z_sum,
    y2_in,
    final,
    z_all,
    mine,
    other,
    feat_send,
    feat_recv,
    bit_send,
    bit_recv,
    relay_send,
    relay_recv,
    head_send,
    head_recv,
    pair_send,
    pair_recv,
    emb_send,
    emb_recv,
    y_send,
    y_recv,
    x_send,
    x_recv,
    z_send,
    z_recv,
    y2_send,
    y2_recv,
    zag_send,
    zag_recv,
    xag_send,
    xag_recv,
    core_send,
    core_recv,
    out_sem,
):
    blk = lax.axis_index("blk")
    f = lax.axis_index("fsdp")
    core = lax.rem(blk, 2)
    z = lax.rem(lax.div(blk, 2), 8)
    x = lax.rem(lax.div(blk, 16), 4)
    yh = lax.div(blk, 64)
    index = blk * 2 + f
    sibling = device_of(x, yh, f, z, 1 - core)
    near = device_of(x, yh, 1 - f, z, core)
    far = device_of(x, 1 - yh, 1 - f, z, core)
    across = device_of(x, 1 - yh, f, z, core)
    x_peers = [device_of(lax.rem(x + k, 4), yh, f, z, core) for k in range(1, 4)]
    z_peers = [device_of(x, yh, f, lax.rem(z + k, 8), core) for k in range(1, 8)]
    step = 3 - 2 * lax.rem(core + f, 2)

    barrier = pltpu.get_barrier_semaphore()

    def hello(device):
        pl.semaphore_signal(barrier, inc=1, device_id=device, device_id_type=MESH)

    for device in [sibling, near, far, across] + x_peers + z_peers:
        hello(device)

    @pl.when(core == 0)
    def _():
        hello(shifted(index, 1))
        hello(shifted(index, 3))

    z_last = lax.div(z, 7)
    z_first = (1 - lax.div(z + 6, 7)) * core
    leaves = z_last * (1 - core)
    turns = z_last * lax.div(x, 3) * core * RELAY
    starts = z_first * (1 - lax.div(x + 2, 3)) * RELAY
    ahead = shifted(index, 32)

    @pl.when(core == 1)
    def _():
        hello(shifted(index, -4))

        @pl.when(z_first == 0)
        def _():
            hello(shifted(index, -6))

        @pl.when(z_first == 1)
        def _():
            hello(device_of(x, yh, f, 7, 0))

    @pl.when(starts == 1)
    def _():
        hello(device_of(3, yh, f, 7, 1))

    @pl.when(leaves == 1)
    def _():
        hello(shifted(index, -32))

    def rows_of(ref, slot):
        start = slot * ROWS
        if not isinstance(slot, int):
            start = pl.multiple_of(start, ROWS)
        return ref.at[pl.ds(start, ROWS)]

    def remote(src, dst, send, recv, device):
        return pltpu.make_async_remote_copy(
            src_ref=src, dst_ref=dst, send_sem=send, recv_sem=recv,
            device_id=device, device_id_type=MESH,
        )

    def feat_copy(src, slot, which, device):
        return remote(src, rows_of(feats, slot), feat_send.at[which], feat_recv.at[slot], device)

    own_half = pl.multiple_of(f * HALF, 16)
    own_pair = pltpu.make_async_copy(pair_ref, pairs.at[0], pair_send.at[0])
    own_pair.start()

    @pl.when(core == 0)
    def _():
        pltpu.make_async_copy(image_ref, rows_of(feats, 0), feat_recv.at[0]).start()
        pltpu.make_async_copy(image_head_ref, head.at[pl.ds(own_half, HALF)], head_recv.at[0]).start()

    @pl.when(core == 1)
    def _():
        pltpu.make_async_copy(text_ref, rows_of(feats, 0), feat_recv.at[0]).start()
        pltpu.make_async_copy(text_head_ref, head.at[pl.ds(own_half, HALF)], head_recv.at[0]).start()

    pl.semaphore_wait(barrier, 16 + leaves + turns)

    def half_rows(half, start, size):
        return pl.ds(pl.multiple_of(half * HALF + start, 16), size)

    def head_copy(src, n, start, size, device):
        return remote(src.at[pl.ds(pl.multiple_of(start, 16), size)], head.at[half_rows(f, start, size)],
                      head_send.at[n], head_recv.at[n + 1], device)

    def head_copies(src):
        return (
            head_copy(src, 1, DIRECT + SHARE * x, SHARE_FAR, far),
            head_copy(src, 2, DIRECT + SHARE * x + SHARE_FAR, SHARE_NEAR, near),
            head_copy(src, 0, 0, DIRECT, far),
        )

    def share_rows(owner, n):
        start = DIRECT + SHARE * owner + n * SHARE_FAR
        return half_rows(1 - f, start, (SHARE_FAR, SHARE_NEAR)[n])

    def share_copy(n, k):
        rows = share_rows(x, n)
        return remote(head.at[rows], head.at[rows], head_send.at[3 + 3 * n + k - 1],
                      head_recv.at[4 + 3 * n + k - 1], x_peers[k - 1])

    pair_copy = remote(pair_ref, pairs.at[1], pair_send.at[1], pair_recv, sibling)

    def bit_copy(src, src_slot, n, slot, device):
        start = slot * ROWS + n * BIT
        return remote(src.at[pl.ds(src_slot * ROWS + n * BIT, BIT)], feats.at[pl.ds(start, BIT)],
                      bit_send.at[slot // 4, n], bit_recv.at[slot - 2, n], device)

    def relay_in(src, n, device):
        rows = pl.ds(n * BIT, BIT)
        return remote(src.at[rows], relay.at[rows], bit_send.at[0, n], relay_recv.at[n], device)

    def relay_on(n, slot, device):
        return remote(relay.at[pl.ds(n * BIT, BIT)], feats.at[pl.ds(slot * ROWS + n * BIT, BIT)],
                      relay_send.at[n], bit_recv.at[slot - 2, n], device)

    def bit_wait(slot, n):
        bit_copy(feats, slot, n, slot, across).wait_recv()

    @pl.when(core == 0)
    def _():


        @pl.when(leaves == 0)
        def _():
            for n in range(BITS):
                bit_copy(text_ref, 0, n, 3, shifted(index, 6)).start()

        @pl.when(leaves == 1)
        def _():
            for n in range(BITS):
                relay_in(text_ref, n, ahead).start()

        for copy in head_copies(image_head_ref):
            copy.start()
        feat_copy(image_ref, step, 0, shifted(index, -step)).start()
        feat_copy(text_ref, 1, 1, sibling).start()

    @pl.when(core == 1)
    def _():

        @pl.when(turns == 0)
        def _():
            for n in range(BITS):
                bit_copy(text_ref, 0, n, 2, shifted(index, 4)).start()

        @pl.when(turns == 1)
        def _():
            for n in range(BITS):
                relay_in(text_ref, n, across).start()

        for copy in head_copies(text_head_ref):
            copy.start()
        feat_copy(image_ref, step, 0, shifted(index, -step)).start()
        feat_copy(image_ref, 2, 1, sibling).start()

    pair_copy.start()

    grad[...] = jnp.zeros_like(grad)

    @pl.when(core == 0)
    def _():
        rows_of(feats, 4)[...] = jnp.zeros((ROWS, E), jnp.bfloat16)
        rows_of(raw_grad, 4)[...] = jnp.zeros((ROWS, E), jnp.bfloat16)

    own_pair.wait()
    pair_copy.wait()
    signs[2] = jnp.ones((ROWS, ROWS), jnp.float32)
    for which in range(2):
        hit = lax.broadcasted_iota(jnp.int32, (ROWS, ROWS), 0) == pairs[which]
        sign = jnp.where(hit, -1.0, 1.0).astype(jnp.float32)

        @pl.when(core == 0)
        def _():
            signs[which] = sign.T

        @pl.when(core == 1)
        def _():
            signs[1 - which] = sign

    def feat_wait(slot):
        pltpu.make_async_copy(rows_of(feats, slot), rows_of(feats, slot), feat_recv.at[slot]).wait()

    def turn(slot):
        feats_t[:, slot * ROWS : (slot + 1) * ROWS] = rows_of(feats, slot)[...].T

    def head_wait(rows, sem):
        pltpu.make_async_copy(head.at[rows], head.at[rows], head_recv.at[sem]).wait()

    other_half = pl.multiple_of((1 - f) * HALF, 16)

    for n in range(2):
        head_wait(share_rows(x, n), 2 + n)
        for k in range(1, 4):
            share_copy(n, k).start()

    for n in range(BITS):
        @pl.when(leaves == 1)
        def _():
            relay_in(text_ref, n, ahead).wait_recv()
            relay_on(n, 3, device_of(x, yh, f, 0, 1)).start()

        @pl.when(turns == 1)
        def _():
            relay_in(text_ref, n, across).wait_recv()
            relay_on(n, 2, device_of(0, yh, f, 0, 1)).start()

        @pl.when(core == 1)
        def _():
            bit_wait(2, n)
            bit_copy(feats, 2, n, 4, shifted(index, 4)).start()

    @pl.when(core == 0)
    def _():
        feat_wait(2)

    for slot in (0, 1):
        feat_wait(slot)
    for slot in (0, 1, 2):
        turn(slot)

    head_wait(pl.ds(own_half, HALF), 0)
    head_wait(half_rows(1 - f, 0, DIRECT), 1)
    for n in range(2):
        for k in range(1, 4):
            head_wait(share_rows(lax.rem(x + 4 - k, 4), n), 4 + 3 * n + k - 1)

    def emb_copy(slot):
        return remote(rows_of(emb, slot), rows_of(emb_other, slot),
                      emb_send.at[slot], emb_recv.at[slot], sibling)

    def embed(slot):
        product = jnp.dot(rows_of(feats, slot)[...], head[...], preferred_element_type=jnp.float32)
        inverse = lax.rsqrt(jnp.sum(product * product, axis=1, keepdims=True) + 1e-06)
        unit = product * inverse
        rows_of(raw, slot)[...] = unit
        rows_of(inv, slot)[...] = inverse
        rows_of(emb, slot)[...] = unit.astype(jnp.bfloat16)
        emb_copy(slot).start()

    def embed_step(slot, carry):
        @pl.when((slot == 3) & (core == 0))
        def _():
            feat_wait(3)

        @pl.when((slot == 3) & (core == 1))
        def _():
            for n in range(BITS):
                bit_wait(3, n)

        embed(slot)
        return carry

    lax.fori_loop(0, 4, embed_step, 0)

    @pl.when(core == 1)
    def _():
        for n in range(BITS):
            bit_wait(4, n)
        embed(4)

    turn(3)
    turn(4)

    for slot in range(4):
        @pl.when(core == 0)
        def _():
            emb_copy(slot).wait_recv()

        @pl.when(core == 1)
        def _():
            emb_copy(slot).wait_recv()

    @pl.when(core == 0)
    def _():
        emb_copy(4).wait_recv()

    scale = scale_ref[0]
    bias = bias_ref[0]

    def item(n, carry):
        at0 = lax.div(n, 2)
        at1 = lax.div(n + 1, 2)
        col0 = 1 - lax.div(at0, 2) + 2 * lax.rem(n, 2)
        col1 = 2 * lax.rem(n + 1, 2)
        at = at0 + core * (at1 - at0)
        col = col0 + core * (col1 - col0)
        kind = 2 - (
            is_equal(n, 0) * (2 - core) + is_equal(n, 4) * (1 - core) + is_equal(n, 1) * 2 * core
        )
        block = emb_other[pl.ds(pl.multiple_of(col * ROWS, ROWS), 2 * ROWS)]
        scores = scale * lax.dot_general(
            rows_of(emb, at)[...], block, (((1,), (1,)), ((), ())),
            preferred_element_type=jnp.float32,
        ) + bias
        sign = signs[kind]
        first = sign * (0.0625 + 0.0625 * jnp.tanh((0.5 * sign) * scores[:, :ROWS]))
        second = 0.0625 + 0.0625 * jnp.tanh(0.5 * scores[:, ROWS:])
        slope = jnp.concatenate([first, second], axis=1).astype(jnp.bfloat16)
        here = rows_of(grad, at)
        here[...] += jnp.dot(slope, block, preferred_element_type=jnp.float32)
        return carry

    lax.fori_loop(0, 8, item, 0)

    def finish(slot, carry):
        unit = rows_of(raw, slot)[...]
        slope = scale * rows_of(grad, slot)[...]
        inner = jnp.sum(unit * slope, axis=1, keepdims=True)
        rows_of(raw_grad, slot)[...] = (
            (slope - unit * inner) * rows_of(inv, slot)[...]
        ).astype(jnp.bfloat16)
        return carry

    lax.fori_loop(0, 4, finish, 0)

    @pl.when(core == 1)
    def _():
        finish(4, 0)

    SIDE = HALF // 2

    def cols_of(j):
        return pl.ds(STARTS[j], WIDTHS[j])

    def wide_of(j):
        return pl.ds(STARTS[j] + 128 * j, WIDTHS[j] + 128)

    def main_of(j):
        return pl.ds(STARTS[j] + 128 * j, WIDTHS[j])

    def rest_of(j):
        return pl.ds(STARTS[j] + 128 * j + WIDTHS[j], 128)

    def y_copies(j):
        cols = cols_of(j)
        return (
            remote(y_out.at[pl.ds(0, SIDE), cols], y_in.at[pl.ds(0, SIDE), cols],
                   y_send.at[j, 0], y_recv.at[j, 0], near),
            remote(y_out.at[pl.ds(SIDE, SIDE), cols], y_in.at[pl.ds(SIDE, SIDE), cols],
                   y_send.at[j, 1], y_recv.at[j, 1], far),
        )

    for j in range(PARTS):
        cols = cols_of(j)
        y_out[:, cols] = jnp.dot(
            feats_t[pl.ds(other_half, HALF), :], raw_grad[:, cols], preferred_element_type=jnp.float32
        ).astype(jnp.bfloat16)
        for copy in y_copies(j):
            copy.start()
    for j in range(PARTS):
        cols = cols_of(j)
        total[:, cols] = jnp.dot(
            feats_t[pl.ds(own_half, HALF), :], raw_grad[:, cols], preferred_element_type=jnp.float32
        )

    def x_copy(j, k):
        cols = cols_of(j)
        return remote(x_out.at[k - 1, :, cols], x_in.at[k - 1, :, cols],
                      x_send.at[j, k - 1], x_recv.at[j, k - 1], x_peers[k - 1])

    def z_copy(j, k):
        cols = wide_of(j)
        return remote(z_out.at[k - 1, :, cols], z_in.at[k - 1, :, cols],
                      z_send.at[j, k - 1], z_recv.at[j, k - 1], z_peers[k - 1])

    def y2_copy(j):
        cols = wide_of(j)
        return remote(z_sum.at[:, cols], y2_in.at[:, cols], y2_send.at[j], y2_recv.at[j], across)

    def zag_copy(j, k):
        cols = wide_of(j)
        return remote(final.at[:, cols], z_all.at[k - 1, :, cols],
                      zag_send.at[j, k - 1], zag_recv.at[j, k - 1], z_peers[k - 1])

    def x_rows(at):
        return pl.ds(pl.multiple_of(at * XROWS, 16), XROWS)

    def xag_copy(j, k, at):
        rows, cols = x_rows(at), cols_of(j)
        return remote(mine.at[rows, cols], mine.at[rows, cols],
                      xag_send.at[j, k - 1], xag_recv.at[j, k - 1], x_peers[k - 1])

    def core_copy(j):
        cols = cols_of(j)
        return remote(mine.at[:, cols], other.at[:, cols], core_send.at[j], core_recv.at[j], sibling)

    def stage_a(j):
        cols = cols_of(j)
        for copy in y_copies(j):
            copy.wait_recv()
        for k in range(1, 4):
            rows = x_rows(lax.rem(x + k, 4))
            x_out[k - 1, :, cols] = (
                total[rows, cols] + y_in[rows, cols].astype(jnp.float32)
            ).astype(jnp.bfloat16)
            x_copy(j, k).start()
        x_sum[:, cols] = total[x_rows(x), cols] + y_in[x_rows(x), cols].astype(jnp.float32)

    def extra_cols(j, at):
        block = lax.div(at * (WIDTHS[j] // 128), 8)
        return pl.ds(pl.multiple_of(STARTS[j] + block * 128, 128), 128)

    def piece_rows(at):
        return pl.ds(pl.multiple_of(at * PIECE, PIECE), PIECE)

    def stage_b(j):
        cols = cols_of(j)
        for k in range(1, 4):
            x_copy(j, k).wait_recv()
        x_sum[:, cols] = (
            x_sum[:, cols] + x_in[0, :, cols].astype(jnp.float32)
        ) + (x_in[1, :, cols].astype(jnp.float32) + x_in[2, :, cols].astype(jnp.float32))
        for k in range(1, 8):
            at = lax.rem(z + k, 8)
            z_out[k - 1, :, main_of(j)] = x_sum[piece_rows(at), cols].astype(jnp.bfloat16)
            z_out[k - 1, :, rest_of(j)] = x_sum[8 * PIECE :, extra_cols(j, at)].astype(jnp.bfloat16)
            z_copy(j, k).start()
        z_sum[:, main_of(j)] = x_sum[piece_rows(z), cols]
        z_sum[:, rest_of(j)] = x_sum[8 * PIECE :, extra_cols(j, z)]

    def stage_c(j):
        cols = wide_of(j)
        for k in range(1, 8):
            z_copy(j, k).wait_recv()
        acc = z_sum[:, cols]
        for k in range(1, 8):
            acc = acc + z_in[k - 1, :, cols].astype(jnp.float32)
        z_sum[:, cols] = acc
        y2_copy(j).start()

    def place(j, at, piece):
        rows = pl.ds(pl.multiple_of(x * XROWS + at * PIECE, PIECE), PIECE)
        mine[rows, cols_of(j)] = piece[:, : WIDTHS[j]]
        tail = pl.ds(pl.multiple_of(x * XROWS + 8 * PIECE, PIECE), PIECE)
        blocks = WIDTHS[j] // 128
        for n in range(blocks):
            @pl.when(at == -(-8 * n // blocks))
            def _():
                mine[tail, pl.ds(STARTS[j] + n * 128, 128)] = piece[:, WIDTHS[j] :]

    def stage_d(j):
        cols = wide_of(j)
        y2_copy(j).wait_recv()
        final[:, cols] = (z_sum[:, cols] + y2_in[:, cols]).astype(jnp.bfloat16)
        for k in range(1, 8):
            zag_copy(j, k).start()
        place(j, z, final[:, cols])

    def stage_e(j):
        for k in range(1, 8):
            zag_copy(j, k).wait_recv()
            place(j, lax.rem(z + 8 - k, 8), z_all[k - 1, :, wide_of(j)])
        for k in range(1, 4):
            xag_copy(j, k, x).start()

    def stage_f(j):
        for k in range(1, 4):
            xag_copy(j, k, lax.rem(x + 4 - k, 4)).wait_recv()
        core_copy(j).start()

    def out_copies(j, first, second):
        cols = cols_of(j)
        return (
            pltpu.make_async_copy(mine.at[:, cols], first.at[:, cols], out_sem.at[j, 0]),
            pltpu.make_async_copy(other.at[:, cols], second.at[:, cols], out_sem.at[j, 1]),
        )

    def stage_g(j):
        core_copy(j).wait_recv()

        @pl.when(core == 0)
        def _():
            for copy in out_copies(j, image_out, text_out):
                copy.start()

        @pl.when(core == 1)
        def _():
            for copy in out_copies(j, text_out, image_out):
                copy.start()

    stages = (stage_a, stage_b, stage_c, stage_d, stage_e, stage_f, stage_g)
    for turn_at in range(len(stages) + PARTS - 1):
        for j in range(PARTS):
            if 0 <= turn_at - j < len(stages):
                stages[turn_at - j](j)

    for copy in head_copies(image_head_ref):
        copy.wait_send()
    for n in range(2):
        for k in range(1, 4):
            share_copy(n, k).wait_send()

    for which in range(2):
        feat_copy(image_ref, 0, which, sibling).wait_send()
    for n in range(BITS):
        bit_copy(text_ref, 0, n, 2, across).wait_send()

    @pl.when(core == 1)
    def _():
        for n in range(BITS):
            bit_copy(feats, 2, n, 4, across).wait_send()
        emb_copy(4).wait_send()

    @pl.when(leaves + turns == 1)
    def _():
        for n in range(BITS):
            relay_on(n, 2, across).wait_send()

    for slot in range(4):
        emb_copy(slot).wait_send()
    for j in range(PARTS):
        for copy in y_copies(j):
            copy.wait_send()
        for k in range(1, 4):
            x_copy(j, k).wait_send()
            xag_copy(j, k, x).wait_send()
        for k in range(1, 8):
            z_copy(j, k).wait_send()
            zag_copy(j, k).wait_send()
        y2_copy(j).wait_send()
        core_copy(j).wait_send()
        for copy in out_copies(j, image_out, text_out):
            copy.wait()


def on_device(
    image_features, text_features, image_head, text_head, pair_index, logit_scale, logit_bias
):
    hbm = pl.BlockSpec(memory_space=pl.ANY)
    smem = pl.BlockSpec(memory_space=pltpu.SMEM)
    bf16, f32 = jnp.bfloat16, jnp.float32
    vmem = pltpu.VMEM
    dma = pltpu.SemaphoreType.DMA
    image_half, text_half = pl.pallas_call(
        kernel,
        out_shape=(
            jax.ShapeDtypeStruct((HALF, E), bf16),
            jax.ShapeDtypeStruct((HALF, E), bf16),
        ),
        in_specs=[hbm, hbm, hbm, hbm, hbm, smem, smem],
        out_specs=(hbm, hbm),
        scratch_shapes=[
            vmem((SLOTS * ROWS, E), bf16),
            vmem((E, SLOTS * ROWS), bf16),
            vmem((E, E), bf16),
            vmem((SLOTS * ROWS, E), f32),
            vmem((SLOTS * ROWS, 1), f32),
            vmem((SLOTS * ROWS, E), bf16),
            vmem((SLOTS * ROWS, E), bf16),
            vmem((SLOTS * ROWS, E), f32),
            vmem((SLOTS * ROWS, E), bf16),
            vmem((ROWS, E), bf16),
            vmem((2, 1, ROWS), jnp.int32),
            vmem((3, ROWS, ROWS), f32),
            vmem((HALF, E), bf16),
            vmem((HALF, E), bf16),
            vmem((HALF, E), f32),
            vmem((3, XROWS, E), bf16),
            vmem((3, XROWS, E), bf16),
            vmem((XROWS, E), f32),
            vmem((7, PIECE, PWIDE), bf16),
            vmem((7, PIECE, PWIDE), bf16),
            vmem((PIECE, PWIDE), f32),
            vmem((PIECE, PWIDE), f32),
            vmem((PIECE, PWIDE), bf16),
            vmem((7, PIECE, PWIDE), bf16),
            vmem((HALF, E), bf16),
            vmem((HALF, E), bf16),
            dma((2,)),
            dma((SLOTS,)),
            dma((2, BITS)),
            dma((3, BITS)),
            dma((BITS,)),
            dma((BITS,)),
            dma((9,)),
            dma((10,)),
            dma((2,)),
            dma,
            dma((SLOTS,)),
            dma((SLOTS,)),
            dma((PARTS, 2)),
            dma((PARTS, 2)),
            dma((PARTS, 3)),
            dma((PARTS, 3)),
            dma((PARTS, 7)),
            dma((PARTS, 7)),
            dma((PARTS,)),
            dma((PARTS,)),
            dma((PARTS, 7)),
            dma((PARTS, 7)),
            dma((PARTS, 3)),
            dma((PARTS, 3)),
            dma((PARTS,)),
            dma((PARTS,)),
            dma((PARTS, 2)),
        ],
        compiler_params=pltpu.CompilerParams(
            collective_id=0, has_side_effects=True, vmem_limit_bytes=60 * 2**20
        ),
        cost_estimate=pl.CostEstimate(
            flops=12 * 10**9, bytes_accessed=12 * 10**6, transcendentals=10**6
        ),
    )(image_features, text_features, image_head, text_head, pair_index, logit_scale, logit_bias)
    return (image_half.astype(f32), text_half.astype(f32))


def solution(mesh):
    placed = (
        P(("blk", "fsdp"), None),
        P(("blk", "fsdp"), None),
        P("fsdp", None),
        P("fsdp", None),
        P(("blk", "fsdp"), None),
        P(),
        P(),
    )
    return jax.shard_map(
        on_device,
        mesh=mesh,
        in_specs=placed,
        out_specs=(P("fsdp", None), P("fsdp", None)),
        check_vma=False,
    )
```

```python
import jax
import jax.numpy as jnp
from jax import lax
from jax.experimental import pallas as pl
from jax.experimental.pallas import tpu as pltpu
from jax.sharding import PartitionSpec as P

STEPS = 8
MESH = pl.DeviceIdType.MESH
ROWS = 256
E = 1152
HALF = E // 2
SLOTS = 5
EARLY = 512
WIDEN = 2
WIDTHS = (384, 384, 384)
PARTS = len(WIDTHS)
STARTS = tuple(sum(WIDTHS[:n]) for n in range(PARTS))
BITS = 4
RELAY = 0
BIT = ROWS // BITS
DIRECT = 192
SHARE = (HALF - DIRECT) // 4
SHARE_FAR = 64
SHARE_NEAR = SHARE - SHARE_FAR
XROWS = HALF // 4
PIECE = 16
PWIDE = E + 128 * PARTS


def device_of(x, yh, f, z, core):
    return (((yh * 4 + x) * 8 + z) * 2 + core, f)


def shifted(index, by):
    other = lax.rem(index + (by + 256), 256)
    return (lax.div(other, 2), lax.rem(other, 2))


def is_equal(n, k):
    gap = n - k
    return 1 - lax.div(gap * gap + 99, 100)


def kernel(
    image_ref,
    text_ref,
    image_head_ref,
    text_head_ref,
    pair_ref,
    scale_ref,
    bias_ref,
    image_out,
    text_out,
    feats,
    feats_t,
    head,
    raw,
    inv,
    emb,
    emb_other,
    grad,
    raw_grad,
    relay,
    pairs,
    signs,
    y_out,
    y_in,
    total,
    x_out,
    x_in,
    x_sum,
    z_out,
    z_in,
    z_sum,
    y2_in,
    final,
    z_all,
    mine,
    other,
    feat_send,
    feat_recv,
    bit_send,
    bit_recv,
    relay_send,
    relay_recv,
    head_send,
    head_recv,
    pair_send,
    pair_recv,
    emb_send,
    emb_recv,
    y_send,
    y_recv,
    x_send,
    x_recv,
    z_send,
    z_recv,
    y2_send,
    y2_recv,
    zag_send,
    zag_recv,
    xag_send,
    xag_recv,
    core_send,
    core_recv,
    out_sem,
):
    blk = lax.axis_index("blk")
    f = lax.axis_index("fsdp")
    core = lax.rem(blk, 2)
    z = lax.rem(lax.div(blk, 2), 8)
    x = lax.rem(lax.div(blk, 16), 4)
    yh = lax.div(blk, 64)
    index = blk * 2 + f
    sibling = device_of(x, yh, f, z, 1 - core)
    near = device_of(x, yh, 1 - f, z, core)
    far = device_of(x, 1 - yh, 1 - f, z, core)
    across = device_of(x, 1 - yh, f, z, core)
    x_peers = [device_of(lax.rem(x + k, 4), yh, f, z, core) for k in range(1, 4)]
    z_peers = [device_of(x, yh, f, lax.rem(z + k, 8), core) for k in range(1, 8)]
    step = 3 - 2 * lax.rem(core + f, 2)

    barrier = pltpu.get_barrier_semaphore()

    def hello(device):
        pl.semaphore_signal(barrier, inc=1, device_id=device, device_id_type=MESH)

    for device in [sibling, near, far, across] + x_peers + z_peers:
        hello(device)

    @pl.when(core == 0)
    def _():
        hello(shifted(index, 1))
        hello(shifted(index, 3))

    z_last = lax.div(z, 7)
    z_first = (1 - lax.div(z + 6, 7)) * core
    leaves = z_last * (1 - core)
    turns = z_last * lax.div(x, 3) * core * RELAY
    starts = z_first * (1 - lax.div(x + 2, 3)) * RELAY
    ahead = shifted(index, 32)

    @pl.when(core == 1)
    def _():
        hello(shifted(index, -4))

        @pl.when(z_first == 0)
        def _():
            hello(shifted(index, -6))

        @pl.when(z_first == 1)
        def _():
            hello(device_of(x, yh, f, 7, 0))

    @pl.when(starts == 1)
    def _():
        hello(device_of(3, yh, f, 7, 1))

    @pl.when(leaves == 1)
    def _():
        hello(shifted(index, -32))

    def rows_of(ref, slot):
        start = slot * ROWS
        if not isinstance(slot, int):
            start = pl.multiple_of(start, ROWS)
        return ref.at[pl.ds(start, ROWS)]

    def remote(src, dst, send, recv, device):
        return pltpu.make_async_remote_copy(
            src_ref=src, dst_ref=dst, send_sem=send, recv_sem=recv,
            device_id=device, device_id_type=MESH,
        )

    def feat_copy(src, slot, which, device):
        return remote(src, rows_of(feats, slot), feat_send.at[which], feat_recv.at[slot], device)

    own_half = pl.multiple_of(f * HALF, 16)
    own_pair = pltpu.make_async_copy(pair_ref, pairs.at[0], pair_send.at[0])
    own_pair.start()

    @pl.when(core == 0)
    def _():
        pltpu.make_async_copy(image_ref, rows_of(feats, 0), feat_recv.at[0]).start()
        pltpu.make_async_copy(image_head_ref, head.at[pl.ds(own_half, HALF)], head_recv.at[0]).start()

    @pl.when(core == 1)
    def _():
        pltpu.make_async_copy(text_ref, rows_of(feats, 0), feat_recv.at[0]).start()
        pltpu.make_async_copy(text_head_ref, head.at[pl.ds(own_half, HALF)], head_recv.at[0]).start()

    pl.semaphore_wait(barrier, 16 + leaves + turns)

    def half_rows(half, start, size):
        return pl.ds(pl.multiple_of(half * HALF + start, 16), size)

    def head_copy(src, n, start, size, device):
        return remote(src.at[pl.ds(pl.multiple_of(start, 16), size)], head.at[half_rows(f, start, size)],
                      head_send.at[n], head_recv.at[n + 1], device)

    def head_copies(src):
        return (
            head_copy(src, 1, DIRECT + SHARE * x, SHARE_FAR, far),
            head_copy(src, 2, DIRECT + SHARE * x + SHARE_FAR, SHARE_NEAR, near),
            head_copy(src, 0, 0, DIRECT, far),
        )

    def share_rows(owner, n):
        start = DIRECT + SHARE * owner + n * SHARE_FAR
        return half_rows(1 - f, start, (SHARE_FAR, SHARE_NEAR)[n])

    def share_copy(n, k):
        rows = share_rows(x, n)
        return remote(head.at[rows], head.at[rows], head_send.at[3 + 3 * n + k - 1],
                      head_recv.at[4 + 3 * n + k - 1], x_peers[k - 1])

    pair_copy = remote(pair_ref, pairs.at[1], pair_send.at[1], pair_recv, sibling)

    def bit_copy(src, src_slot, n, slot, device):
        start = slot * ROWS + n * BIT
        return remote(src.at[pl.ds(src_slot * ROWS + n * BIT, BIT)], feats.at[pl.ds(start, BIT)],
                      bit_send.at[slot // 4, n], bit_recv.at[slot - 2, n], device)

    def relay_in(src, n, device):
        rows = pl.ds(n * BIT, BIT)
        return remote(src.at[rows], relay.at[rows], bit_send.at[0, n], relay_recv.at[n], device)

    def relay_on(n, slot, device):
        return remote(relay.at[pl.ds(n * BIT, BIT)], feats.at[pl.ds(slot * ROWS + n * BIT, BIT)],
                      relay_send.at[n], bit_recv.at[slot - 2, n], device)

    def bit_wait(slot, n):
        bit_copy(feats, slot, n, slot, across).wait_recv()

    @pl.when(core == 0)
    def _():


        @pl.when(leaves == 0)
        def _():
            for n in range(BITS):
                bit_copy(text_ref, 0, n, 3, shifted(index, 6)).start()

        @pl.when(leaves == 1)
        def _():
            for n in range(BITS):
                relay_in(text_ref, n, ahead).start()

        for copy in head_copies(image_head_ref):
            copy.start()
        feat_copy(image_ref, step, 0, shifted(index, -step)).start()
        feat_copy(text_ref, 1, 1, sibling).start()

    @pl.when(core == 1)
    def _():

        @pl.when(turns == 0)
        def _():
            for n in range(BITS):
                bit_copy(text_ref, 0, n, 2, shifted(index, 4)).start()

        @pl.when(turns == 1)
        def _():
            for n in range(BITS):
                relay_in(text_ref, n, across).start()

        for copy in head_copies(text_head_ref):
            copy.start()
        feat_copy(image_ref, step, 0, shifted(index, -step)).start()
        feat_copy(image_ref, 2, 1, sibling).start()

    pair_copy.start()

    grad[...] = jnp.zeros_like(grad)

    @pl.when(core == 0)
    def _():
        rows_of(feats, 4)[...] = jnp.zeros((ROWS, E), jnp.bfloat16)
        rows_of(raw_grad, 4)[...] = jnp.zeros((ROWS, E), jnp.bfloat16)

    own_pair.wait()
    pair_copy.wait()
    signs[2] = jnp.ones((ROWS, ROWS), jnp.float32)
    for which in range(2):
        hit = lax.broadcasted_iota(jnp.int32, (ROWS, ROWS), 0) == pairs[which]
        sign = jnp.where(hit, -1.0, 1.0).astype(jnp.float32)

        @pl.when(core == 0)
        def _():
            signs[which] = sign.T

        @pl.when(core == 1)
        def _():
            signs[1 - which] = sign

    def feat_wait(slot):
        pltpu.make_async_copy(rows_of(feats, slot), rows_of(feats, slot), feat_recv.at[slot]).wait()

    def turn(slot):
        feats_t[:, slot * ROWS : (slot + 1) * ROWS] = rows_of(feats, slot)[...].T

    def head_wait(rows, sem):
        pltpu.make_async_copy(head.at[rows], head.at[rows], head_recv.at[sem]).wait()

    other_half = pl.multiple_of((1 - f) * HALF, 16)

    for n in range(2):
        head_wait(share_rows(x, n), 2 + n)
        for k in range(1, 4):
            share_copy(n, k).start()

    for n in range(BITS):
        @pl.when(leaves == 1)
        def _():
            relay_in(text_ref, n, ahead).wait_recv()
            relay_on(n, 3, device_of(x, yh, f, 0, 1)).start()

        @pl.when(turns == 1)
        def _():
            relay_in(text_ref, n, across).wait_recv()
            relay_on(n, 2, device_of(0, yh, f, 0, 1)).start()

        @pl.when(core == 1)
        def _():
            bit_wait(2, n)
            bit_copy(feats, 2, n, 4, shifted(index, 4)).start()

    @pl.when(core == 0)
    def _():
        feat_wait(2)

    for slot in (0, 1):
        feat_wait(slot)

    head_wait(pl.ds(own_half, HALF), 0)
    early = pl.ds(pl.multiple_of(f * (E - EARLY), 128), EARLY)
    late = pl.ds(pl.multiple_of((1 - f) * EARLY, 128), E - EARLY)

    def begin(slot, carry):
        rows_of(raw, slot)[...] = jnp.dot(
            rows_of(feats, slot)[:, early], head[early, :], preferred_element_type=jnp.float32
        )
        return carry

    lax.fori_loop(0, 3, begin, 0)
    for slot in (0, 1, 2):
        turn(slot)

    head_wait(half_rows(1 - f, 0, DIRECT), 1)
    for n in range(2):
        for k in range(1, 4):
            head_wait(share_rows(lax.rem(x + 4 - k, 4), n), 4 + 3 * n + k - 1)

    def emb_copy(slot):
        return remote(rows_of(emb, slot), rows_of(emb_other, slot),
                      emb_send.at[slot], emb_recv.at[slot], sibling)

    def embed(slot):
        product = rows_of(raw, slot)[...] + jnp.dot(
            rows_of(feats, slot)[:, late], head[late, :], preferred_element_type=jnp.float32
        )
        inverse = lax.rsqrt(jnp.sum(product * product, axis=1, keepdims=True) + 1e-06)
        unit = product * inverse
        rows_of(raw, slot)[...] = unit
        rows_of(inv, slot)[...] = inverse
        rows_of(emb, slot)[...] = unit.astype(jnp.bfloat16)
        emb_copy(slot).start()

    def embed_step(slot, carry):
        @pl.when((slot == 3) & (core == 0))
        def _():
            feat_wait(3)

        @pl.when((slot == 3) & (core == 1))
        def _():
            for n in range(BITS):
                bit_wait(3, n)

        @pl.when(slot == 3)
        def _():
            begin(3, 0)

        embed(slot)
        return carry

    lax.fori_loop(0, 4, embed_step, 0)

    @pl.when(core == 1)
    def _():
        for n in range(BITS):
            bit_wait(4, n)
        begin(4, 0)
        embed(4)

    turn(3)
    turn(4)

    for slot in range(4):
        @pl.when(core == 0)
        def _():
            emb_copy(slot).wait_recv()

        @pl.when(core == 1)
        def _():
            emb_copy(slot).wait_recv()

    @pl.when(core == 0)
    def _():
        emb_copy(4).wait_recv()

    scale = scale_ref[0]
    bias = bias_ref[0]

    def item(n, carry):
        at0 = lax.div(n, 2)
        at1 = lax.div(n + 1, 2)
        col0 = 1 - lax.div(at0, 2) + 2 * lax.rem(n, 2)
        col1 = 2 * lax.rem(n + 1, 2)
        at = at0 + core * (at1 - at0)
        col = col0 + core * (col1 - col0)
        kind = 2 - (
            is_equal(n, 0) * (2 - core) + is_equal(n, 4) * (1 - core) + is_equal(n, 1) * 2 * core
        )
        block = emb_other[pl.ds(pl.multiple_of(col * ROWS, ROWS), 2 * ROWS)]
        scores = scale * lax.dot_general(
            rows_of(emb, at)[...], block, (((1,), (1,)), ((), ())),
            preferred_element_type=jnp.float32,
        ) + bias
        sign = signs[kind]
        first = sign * (0.0625 + 0.0625 * jnp.tanh((0.5 * sign) * scores[:, :ROWS]))
        second = 0.0625 + 0.0625 * jnp.tanh(0.5 * scores[:, ROWS:])
        slope = jnp.concatenate([first, second], axis=1).astype(jnp.bfloat16)
        here = rows_of(grad, at)
        here[...] += jnp.dot(slope, block, preferred_element_type=jnp.float32)
        return carry

    lax.fori_loop(0, 8, item, 0)

    def finish(slot, carry):
        unit = rows_of(raw, slot)[...]
        slope = scale * rows_of(grad, slot)[...]
        inner = jnp.sum(unit * slope, axis=1, keepdims=True)
        rows_of(raw_grad, slot)[...] = (
            (slope - unit * inner) * rows_of(inv, slot)[...]
        ).astype(jnp.bfloat16)
        return carry

    lax.fori_loop(0, 4, finish, 0)

    @pl.when(core == 1)
    def _():
        finish(4, 0)

    SIDE = HALF // 2

    def cols_of(j):
        return pl.ds(STARTS[j], WIDTHS[j])

    def wide_of(j):
        return pl.ds(STARTS[j] + 128 * j, WIDTHS[j] + 128)

    def main_of(j):
        return pl.ds(STARTS[j] + 128 * j, WIDTHS[j])

    def rest_of(j):
        return pl.ds(STARTS[j] + 128 * j + WIDTHS[j], 128)

    def y_copies(j):
        cols = cols_of(j)
        return (
            remote(y_out.at[pl.ds(0, SIDE), cols], y_in.at[pl.ds(0, SIDE), cols],
                   y_send.at[j, 0], y_recv.at[j, 0], near),
            remote(y_out.at[pl.ds(SIDE, SIDE), cols], y_in.at[pl.ds(SIDE, SIDE), cols],
                   y_send.at[j, 1], y_recv.at[j, 1], far),
        )

    for j in range(PARTS):
        cols = cols_of(j)
        y_out[:, cols] = jnp.dot(
            feats_t[pl.ds(other_half, HALF), :], raw_grad[:, cols], preferred_element_type=jnp.float32
        ).astype(jnp.bfloat16)
        for copy in y_copies(j):
            copy.start()
    for j in range(PARTS):
        cols = cols_of(j)
        total[:, cols] = jnp.dot(
            feats_t[pl.ds(own_half, HALF), :], raw_grad[:, cols], preferred_element_type=jnp.float32
        )

    def x_copy(j, k):
        cols = cols_of(j)
        return remote(x_out.at[k - 1, :, cols], x_in.at[k - 1, :, cols],
                      x_send.at[j, k - 1], x_recv.at[j, k - 1], x_peers[k - 1])

    def z_copy(j, k):
        cols = wide_of(j)
        return remote(z_out.at[k - 1, :, cols], z_in.at[k - 1, :, cols],
                      z_send.at[j, k - 1], z_recv.at[j, k - 1], z_peers[k - 1])

    def y2_copy(j):
        cols = wide_of(j)
        return remote(z_sum.at[:, cols], y2_in.at[:, cols], y2_send.at[j], y2_recv.at[j], across)

    def zag_copy(j, k):
        cols = wide_of(j)
        return remote(final.at[:, cols], z_all.at[k - 1, :, cols],
                      zag_send.at[j, k - 1], zag_recv.at[j, k - 1], z_peers[k - 1])

    def x_rows(at):
        return pl.ds(pl.multiple_of(at * XROWS, 16), XROWS)

    def xag_copy(j, k, at):
        rows, cols = x_rows(at), cols_of(j)
        return remote(mine.at[rows, cols], mine.at[rows, cols],
                      xag_send.at[j, k - 1], xag_recv.at[j, k - 1], x_peers[k - 1])

    def core_copy(j):
        cols = cols_of(j)
        return remote(mine.at[:, cols], other.at[:, cols], core_send.at[j], core_recv.at[j], sibling)

    def stage_a(j):
        cols = cols_of(j)
        for copy in y_copies(j):
            copy.wait_recv()
        for k in range(1, 4):
            rows = x_rows(lax.rem(x + k, 4))
            x_out[k - 1, :, cols] = (
                total[rows, cols] + y_in[rows, cols].astype(jnp.float32)
            ).astype(jnp.bfloat16)
            x_copy(j, k).start()
        x_sum[:, cols] = total[x_rows(x), cols] + y_in[x_rows(x), cols].astype(jnp.float32)

    def extra_cols(j, at):
        block = lax.div(at * (WIDTHS[j] // 128), 8)
        return pl.ds(pl.multiple_of(STARTS[j] + block * 128, 128), 128)

    def piece_rows(at):
        return pl.ds(pl.multiple_of(at * PIECE, PIECE), PIECE)

    def stage_b(j):
        cols = cols_of(j)
        for k in range(1, 4):
            x_copy(j, k).wait_recv()
        x_sum[:, cols] = (
            x_sum[:, cols] + x_in[0, :, cols].astype(jnp.float32)
        ) + (x_in[1, :, cols].astype(jnp.float32) + x_in[2, :, cols].astype(jnp.float32))
        for k in range(1, 8):
            at = lax.rem(z + k, 8)
            z_out[k - 1, :, main_of(j)] = x_sum[piece_rows(at), cols].astype(jnp.bfloat16)
            z_out[k - 1, :, rest_of(j)] = x_sum[8 * PIECE :, extra_cols(j, at)].astype(jnp.bfloat16)
            z_copy(j, k).start()
        z_sum[:, main_of(j)] = x_sum[piece_rows(z), cols]
        z_sum[:, rest_of(j)] = x_sum[8 * PIECE :, extra_cols(j, z)]

    def stage_c(j):
        cols = wide_of(j)
        for k in range(1, 8):
            z_copy(j, k).wait_recv()
        acc = z_sum[:, cols]
        for k in range(1, 8):
            acc = acc + z_in[k - 1, :, cols].astype(jnp.float32)
        z_sum[:, cols] = acc
        y2_copy(j).start()

    def place(j, at, piece):
        rows = pl.ds(pl.multiple_of(x * XROWS + at * PIECE, PIECE), PIECE)
        mine[rows, cols_of(j)] = piece[:, : WIDTHS[j]]
        tail = pl.ds(pl.multiple_of(x * XROWS + 8 * PIECE, PIECE), PIECE)
        blocks = WIDTHS[j] // 128
        for n in range(blocks):
            @pl.when(at == -(-8 * n // blocks))
            def _():
                mine[tail, pl.ds(STARTS[j] + n * 128, 128)] = piece[:, WIDTHS[j] :]

    def stage_d(j):
        cols = wide_of(j)
        y2_copy(j).wait_recv()
        final[:, cols] = (z_sum[:, cols] + y2_in[:, cols]).astype(jnp.bfloat16)
        for k in range(1, 8):
            zag_copy(j, k).start()
        place(j, z, final[:, cols])

    def stage_e(j):
        for k in range(1, 8):
            zag_copy(j, k).wait_recv()
            place(j, lax.rem(z + 8 - k, 8), z_all[k - 1, :, wide_of(j)])
        for k in range(1, 4):
            xag_copy(j, k, x).start()

    def stage_f(j):
        for k in range(1, 4):
            xag_copy(j, k, lax.rem(x + 4 - k, 4)).wait_recv()
        core_copy(j).start()

    def out_copies(j, first, second):
        cols = cols_of(j)
        return (
            pltpu.make_async_copy(mine.at[:, cols], first.at[:, cols], out_sem.at[j, 0]),
            pltpu.make_async_copy(other.at[:, cols], second.at[:, cols], out_sem.at[j, 1]),
        )

    def stage_g(j):
        core_copy(j).wait_recv()

        @pl.when(core == 0)
        def _():
            for copy in out_copies(j, image_out, text_out):
                copy.start()

        @pl.when(core == 1)
        def _():
            for copy in out_copies(j, text_out, image_out):
                copy.start()

    stages = (stage_a, stage_b, stage_c, stage_d, stage_e, stage_f, stage_g)
    for turn_at in range(len(stages) + PARTS - 1):
        for j in range(PARTS):
            if 0 <= turn_at - j < len(stages):
                stages[turn_at - j](j)

    for copy in head_copies(image_head_ref):
        copy.wait_send()
    for n in range(2):
        for k in range(1, 4):
            share_copy(n, k).wait_send()

    for which in range(2):
        feat_copy(image_ref, 0, which, sibling).wait_send()
    for n in range(BITS):
        bit_copy(text_ref, 0, n, 2, across).wait_send()

    @pl.when(core == 1)
    def _():
        for n in range(BITS):
            bit_copy(feats, 2, n, 4, across).wait_send()
        emb_copy(4).wait_send()

    @pl.when(leaves + turns == 1)
    def _():
        for n in range(BITS):
            relay_on(n, 2, across).wait_send()

    for slot in range(4):
        emb_copy(slot).wait_send()
    for j in range(PARTS):
        for copy in y_copies(j):
            copy.wait_send()
        for k in range(1, 4):
            x_copy(j, k).wait_send()
            xag_copy(j, k, x).wait_send()
        for k in range(1, 8):
            z_copy(j, k).wait_send()
            zag_copy(j, k).wait_send()
        y2_copy(j).wait_send()
        core_copy(j).wait_send()
        for copy in out_copies(j, image_out, text_out):
            copy.wait()


def widen(image_ref, text_ref, image_out, text_out):
    image_out[...] = image_ref[...].astype(jnp.float32)
    text_out[...] = text_ref[...].astype(jnp.float32)


def on_device(
    image_features, text_features, image_head, text_head, pair_index, logit_scale, logit_bias
):
    hbm = pl.BlockSpec(memory_space=pl.ANY)
    smem = pl.BlockSpec(memory_space=pltpu.SMEM)
    bf16, f32 = jnp.bfloat16, jnp.float32
    vmem = pltpu.VMEM
    dma = pltpu.SemaphoreType.DMA
    image_half, text_half = pl.pallas_call(
        kernel,
        out_shape=(
            jax.ShapeDtypeStruct((HALF, E), bf16),
            jax.ShapeDtypeStruct((HALF, E), bf16),
        ),
        in_specs=[hbm, hbm, hbm, hbm, hbm, smem, smem],
        out_specs=(hbm, hbm),
        scratch_shapes=[
            vmem((SLOTS * ROWS, E), bf16),
            vmem((E, SLOTS * ROWS), bf16),
            vmem((E, E), bf16),
            vmem((SLOTS * ROWS, E), f32),
            vmem((SLOTS * ROWS, 1), f32),
            vmem((SLOTS * ROWS, E), bf16),
            vmem((SLOTS * ROWS, E), bf16),
            vmem((SLOTS * ROWS, E), f32),
            vmem((SLOTS * ROWS, E), bf16),
            vmem((ROWS, E), bf16),
            vmem((2, 1, ROWS), jnp.int32),
            vmem((3, ROWS, ROWS), f32),
            vmem((HALF, E), bf16),
            vmem((HALF, E), bf16),
            vmem((HALF, E), f32),
            vmem((3, XROWS, E), bf16),
            vmem((3, XROWS, E), bf16),
            vmem((XROWS, E), f32),
            vmem((7, PIECE, PWIDE), bf16),
            vmem((7, PIECE, PWIDE), bf16),
            vmem((PIECE, PWIDE), f32),
            vmem((PIECE, PWIDE), f32),
            vmem((PIECE, PWIDE), bf16),
            vmem((7, PIECE, PWIDE), bf16),
            vmem((HALF, E), bf16),
            vmem((HALF, E), bf16),
            dma((2,)),
            dma((SLOTS,)),
            dma((2, BITS)),
            dma((3, BITS)),
            dma((BITS,)),
            dma((BITS,)),
            dma((9,)),
            dma((10,)),
            dma((2,)),
            dma,
            dma((SLOTS,)),
            dma((SLOTS,)),
            dma((PARTS, 2)),
            dma((PARTS, 2)),
            dma((PARTS, 3)),
            dma((PARTS, 3)),
            dma((PARTS, 7)),
            dma((PARTS, 7)),
            dma((PARTS,)),
            dma((PARTS,)),
            dma((PARTS, 7)),
            dma((PARTS, 7)),
            dma((PARTS, 3)),
            dma((PARTS, 3)),
            dma((PARTS,)),
            dma((PARTS,)),
            dma((PARTS, 2)),
        ],
        compiler_params=pltpu.CompilerParams(
            collective_id=0, has_side_effects=True, vmem_limit_bytes=60 * 2**20
        ),
        cost_estimate=pl.CostEstimate(
            flops=12 * 10**9, bytes_accessed=12 * 10**6, transcendentals=10**6
        ),
    )(image_features, text_features, image_head, text_head, pair_index, logit_scale, logit_bias)
    block = pl.BlockSpec((HALF // WIDEN, E), lambda n: (n, 0))
    return pl.pallas_call(
        widen,
        grid=(WIDEN,),
        out_shape=(
            jax.ShapeDtypeStruct((HALF, E), f32),
            jax.ShapeDtypeStruct((HALF, E), f32),
        ),
        in_specs=[block, block],
        out_specs=(block, block),
        compiler_params=pltpu.CompilerParams(vmem_limit_bytes=40 * 2**20),
        cost_estimate=pl.CostEstimate(flops=2 * HALF * E, bytes_accessed=12 * HALF * E, transcendentals=0),
    )(image_half, text_half)


def solution(mesh):
    placed = (
        P(("blk", "fsdp"), None),
        P(("blk", "fsdp"), None),
        P("fsdp", None),
        P("fsdp", None),
        P(("blk", "fsdp"), None),
        P(),
        P(),
    )
    return jax.shard_map(
        on_device,
        mesh=mesh,
        in_specs=placed,
        out_specs=(P("fsdp", None), P("fsdp", None)),
        check_vma=False,
    )
```

```python
import jax
import jax.numpy as jnp
from jax import lax
from jax.experimental import pallas as pl
from jax.experimental.pallas import tpu as pltpu
from jax.sharding import PartitionSpec as P

STEPS = 8
MESH = pl.DeviceIdType.MESH
ROWS = 256
E = 1152
HALF = E // 2
SLOTS = 5
EARLY = 512
WIDEN = 2
WIDTHS = (384, 384, 384)
PARTS = len(WIDTHS)
STARTS = tuple(sum(WIDTHS[:n]) for n in range(PARTS))
BITS = 4
RELAY = 0
BIT = ROWS // BITS
DIRECT = 192
SHARE = (HALF - DIRECT) // 4
SHARE_FAR = 64
SHARE_NEAR = SHARE - SHARE_FAR
XROWS = HALF // 4
PIECE = 16
PWIDE = E + 128 * PARTS


def device_of(x, yh, f, z, core):
    return (((yh * 4 + x) * 8 + z) * 2 + core, f)


def shifted(index, by):
    other = lax.rem(index + (by + 256), 256)
    return (lax.div(other, 2), lax.rem(other, 2))


def is_equal(n, k):
    gap = n - k
    return 1 - lax.div(gap * gap + 99, 100)


def kernel(
    image_ref,
    text_ref,
    image_head_ref,
    text_head_ref,
    pair_ref,
    scale_ref,
    bias_ref,
    image_out,
    text_out,
    feats,
    feats_t,
    head,
    raw,
    inv,
    emb,
    emb_other,
    grad,
    raw_grad,
    relay,
    pairs,
    signs,
    y_out,
    y_in,
    total,
    x_out,
    x_in,
    x_sum,
    z_out,
    z_in,
    z_sum,
    y2_in,
    final,
    z_all,
    mine,
    other,
    feat_send,
    feat_recv,
    bit_send,
    bit_recv,
    relay_send,
    relay_recv,
    head_send,
    head_recv,
    pair_send,
    pair_recv,
    emb_send,
    emb_recv,
    y_send,
    y_recv,
    x_send,
    x_recv,
    z_send,
    z_recv,
    y2_send,
    y2_recv,
    zag_send,
    zag_recv,
    xag_send,
    xag_recv,
    core_send,
    core_recv,
    out_sem,
):
    blk = lax.axis_index("blk")
    f = lax.axis_index("fsdp")
    core = lax.rem(blk, 2)
    z = lax.rem(lax.div(blk, 2), 8)
    x = lax.rem(lax.div(blk, 16), 4)
    yh = lax.div(blk, 64)
    index = blk * 2 + f
    sibling = device_of(x, yh, f, z, 1 - core)
    near = device_of(x, yh, 1 - f, z, core)
    far = device_of(x, 1 - yh, 1 - f, z, core)
    across = device_of(x, 1 - yh, f, z, core)
    x_peers = [device_of(lax.rem(x + k, 4), yh, f, z, core) for k in range(1, 4)]
    z_peers = [device_of(x, yh, f, lax.rem(z + k, 8), core) for k in range(1, 8)]
    step = 3 - 2 * lax.rem(core + f, 2)

    barrier = pltpu.get_barrier_semaphore()

    def hello(device):
        pl.semaphore_signal(barrier, inc=1, device_id=device, device_id_type=MESH)

    for device in [sibling, near, far, across] + x_peers + z_peers:
        hello(device)

    @pl.when(core == 0)
    def _():
        hello(shifted(index, 1))
        hello(shifted(index, 3))

    z_last = lax.div(z, 7)
    z_first = (1 - lax.div(z + 6, 7)) * core
    leaves = z_last * (1 - core)
    turns = z_last * lax.div(x, 3) * core * RELAY
    starts = z_first * (1 - lax.div(x + 2, 3)) * RELAY
    ahead = shifted(index, 32)

    @pl.when(core == 1)
    def _():
        hello(shifted(index, -4))

        @pl.when(z_first == 0)
        def _():
            hello(shifted(index, -6))

        @pl.when(z_first == 1)
        def _():
            hello(device_of(x, yh, f, 7, 0))

    @pl.when(starts == 1)
    def _():
        hello(device_of(3, yh, f, 7, 1))

    @pl.when(leaves == 1)
    def _():
        hello(shifted(index, -32))

    def rows_of(ref, slot):
        start = slot * ROWS
        if not isinstance(slot, int):
            start = pl.multiple_of(start, ROWS)
        return ref.at[pl.ds(start, ROWS)]

    def remote(src, dst, send, recv, device):
        return pltpu.make_async_remote_copy(
            src_ref=src, dst_ref=dst, send_sem=send, recv_sem=recv,
            device_id=device, device_id_type=MESH,
        )

    def feat_copy(src, slot, which, device):
        return remote(src, rows_of(feats, slot), feat_send.at[which], feat_recv.at[slot], device)

    own_half = pl.multiple_of(f * HALF, 16)
    own_pair = pltpu.make_async_copy(pair_ref, pairs.at[0], pair_send.at[0])
    own_pair.start()

    @pl.when(core == 0)
    def _():
        pltpu.make_async_copy(image_ref, rows_of(feats, 0), feat_recv.at[0]).start()
        pltpu.make_async_copy(image_head_ref, head.at[pl.ds(own_half, HALF)], head_recv.at[0]).start()

    @pl.when(core == 1)
    def _():
        pltpu.make_async_copy(text_ref, rows_of(feats, 0), feat_recv.at[0]).start()
        pltpu.make_async_copy(text_head_ref, head.at[pl.ds(own_half, HALF)], head_recv.at[0]).start()

    pl.semaphore_wait(barrier, 16 + leaves + turns)

    def half_rows(half, start, size):
        return pl.ds(pl.multiple_of(half * HALF + start, 16), size)

    def head_copy(src, n, start, size, device):
        return remote(src.at[pl.ds(pl.multiple_of(start, 16), size)], head.at[half_rows(f, start, size)],
                      head_send.at[n], head_recv.at[n + 1], device)

    def head_copies(src):
        return (
            head_copy(src, 1, DIRECT + SHARE * x, SHARE_FAR, far),
            head_copy(src, 2, DIRECT + SHARE * x + SHARE_FAR, SHARE_NEAR, near),
            head_copy(src, 0, 0, DIRECT, far),
        )

    def share_rows(owner, n):
        start = DIRECT + SHARE * owner + n * SHARE_FAR
        return half_rows(1 - f, start, (SHARE_FAR, SHARE_NEAR)[n])

    def share_copy(n, k):
        rows = share_rows(x, n)
        return remote(head.at[rows], head.at[rows], head_send.at[3 + 3 * n + k - 1],
                      head_recv.at[4 + 3 * n + k - 1], x_peers[k - 1])

    pair_copy = remote(pair_ref, pairs.at[1], pair_send.at[1], pair_recv, sibling)

    def bit_copy(src, src_slot, n, slot, device):
        start = slot * ROWS + n * BIT
        return remote(src.at[pl.ds(src_slot * ROWS + n * BIT, BIT)], feats.at[pl.ds(start, BIT)],
                      bit_send.at[slot // 4, n], bit_recv.at[slot - 2, n], device)

    def relay_in(src, n, device):
        rows = pl.ds(n * BIT, BIT)
        return remote(src.at[rows], relay.at[rows], bit_send.at[0, n], relay_recv.at[n], device)

    def relay_on(n, slot, device):
        return remote(relay.at[pl.ds(n * BIT, BIT)], feats.at[pl.ds(slot * ROWS + n * BIT, BIT)],
                      relay_send.at[n], bit_recv.at[slot - 2, n], device)

    def bit_wait(slot, n):
        bit_copy(feats, slot, n, slot, across).wait_recv()

    @pl.when(core == 0)
    def _():


        @pl.when(leaves == 0)
        def _():
            for n in range(BITS):
                bit_copy(text_ref, 0, n, 3, shifted(index, 6)).start()

        @pl.when(leaves == 1)
        def _():
            for n in range(BITS):
                relay_in(text_ref, n, ahead).start()

        for copy in head_copies(image_head_ref):
            copy.start()
        feat_copy(image_ref, step, 0, shifted(index, -step)).start()
        feat_copy(text_ref, 1, 1, sibling).start()

    @pl.when(core == 1)
    def _():

        @pl.when(turns == 0)
        def _():
            for n in range(BITS):
                bit_copy(text_ref, 0, n, 2, shifted(index, 4)).start()

        @pl.when(turns == 1)
        def _():
            for n in range(BITS):
                relay_in(text_ref, n, across).start()

        for copy in head_copies(text_head_ref):
            copy.start()
        feat_copy(image_ref, step, 0, shifted(index, -step)).start()
        feat_copy(image_ref, 2, 1, sibling).start()

    pair_copy.start()

    grad[...] = jnp.zeros_like(grad)

    @pl.when(core == 0)
    def _():
        rows_of(feats, 4)[...] = jnp.zeros((ROWS, E), jnp.bfloat16)
        rows_of(raw_grad, 4)[...] = jnp.zeros((ROWS, E), jnp.bfloat16)

    own_pair.wait()
    pair_copy.wait()
    signs[2] = jnp.ones((ROWS, ROWS), jnp.float32)
    for which in range(2):
        hit = lax.broadcasted_iota(jnp.int32, (ROWS, ROWS), 0) == pairs[which]
        sign = jnp.where(hit, -1.0, 1.0).astype(jnp.float32)

        @pl.when(core == 0)
        def _():
            signs[which] = sign.T

        @pl.when(core == 1)
        def _():
            signs[1 - which] = sign

    def feat_wait(slot):
        pltpu.make_async_copy(rows_of(feats, slot), rows_of(feats, slot), feat_recv.at[slot]).wait()

    def turn(slot):
        feats_t[:, slot * ROWS : (slot + 1) * ROWS] = rows_of(feats, slot)[...].T

    def head_wait(rows, sem):
        pltpu.make_async_copy(head.at[rows], head.at[rows], head_recv.at[sem]).wait()

    other_half = pl.multiple_of((1 - f) * HALF, 16)

    for n in range(2):
        head_wait(share_rows(x, n), 2 + n)
        for k in range(1, 4):
            share_copy(n, k).start()

    for n in range(BITS):
        @pl.when(leaves == 1)
        def _():
            relay_in(text_ref, n, ahead).wait_recv()
            relay_on(n, 3, device_of(x, yh, f, 0, 1)).start()

        @pl.when(turns == 1)
        def _():
            relay_in(text_ref, n, across).wait_recv()
            relay_on(n, 2, device_of(0, yh, f, 0, 1)).start()

        @pl.when(core == 1)
        def _():
            bit_wait(2, n)
            bit_copy(feats, 2, n, 4, shifted(index, 4)).start()

    @pl.when(core == 0)
    def _():
        feat_wait(2)

    for slot in (0, 1):
        feat_wait(slot)

    head_wait(pl.ds(own_half, HALF), 0)
    early = pl.ds(pl.multiple_of(f * (E - EARLY), 128), EARLY)
    late = pl.ds(pl.multiple_of((1 - f) * EARLY, 128), E - EARLY)

    def begin(slot, carry):
        rows_of(raw, slot)[...] = jnp.dot(
            rows_of(feats, slot)[:, early], head[early, :], preferred_element_type=jnp.float32
        )
        return carry

    lax.fori_loop(0, 3, begin, 0)
    for slot in (0, 1, 2):
        turn(slot)

    head_wait(half_rows(1 - f, 0, DIRECT), 1)
    for n in range(2):
        for k in range(1, 4):
            head_wait(share_rows(lax.rem(x + 4 - k, 4), n), 4 + 3 * n + k - 1)

    def emb_copy(slot):
        return remote(rows_of(emb, slot), rows_of(emb_other, slot),
                      emb_send.at[slot], emb_recv.at[slot], sibling)

    def embed(slot):
        product = rows_of(raw, slot)[...] + jnp.dot(
            rows_of(feats, slot)[:, late], head[late, :], preferred_element_type=jnp.float32
        )
        inverse = lax.rsqrt(jnp.sum(product * product, axis=1, keepdims=True) + 1e-06)
        unit = product * inverse
        rows_of(raw, slot)[...] = unit
        rows_of(inv, slot)[...] = inverse
        rows_of(emb, slot)[...] = unit.astype(jnp.bfloat16)
        emb_copy(slot).start()

    def embed_step(slot, carry):
        @pl.when((slot == 3) & (core == 0))
        def _():
            feat_wait(3)

        @pl.when((slot == 3) & (core == 1))
        def _():
            for n in range(BITS):
                bit_wait(3, n)

        @pl.when(slot == 3)
        def _():
            begin(3, 0)

        embed(slot)
        return carry

    lax.fori_loop(0, 4, embed_step, 0)

    @pl.when(core == 1)
    def _():
        for n in range(BITS):
            bit_wait(4, n)
        begin(4, 0)
        embed(4)

    turn(3)
    turn(4)

    for slot in range(4):
        @pl.when(core == 0)
        def _():
            emb_copy(slot).wait_recv()

        @pl.when(core == 1)
        def _():
            emb_copy(slot).wait_recv()

    @pl.when(core == 0)
    def _():
        emb_copy(4).wait_recv()

    scale = scale_ref[0]
    bias = bias_ref[0]

    def item(n, carry):
        at0 = lax.div(n, 2)
        at1 = lax.div(n + 1, 2)
        col0 = 1 - lax.div(at0, 2) + 2 * lax.rem(n, 2)
        col1 = 2 * lax.rem(n + 1, 2)
        at = at0 + core * (at1 - at0)
        col = col0 + core * (col1 - col0)
        kind = 2 - (
            is_equal(n, 0) * (2 - core) + is_equal(n, 4) * (1 - core) + is_equal(n, 1) * 2 * core
        )
        block = emb_other[pl.ds(pl.multiple_of(col * ROWS, ROWS), 2 * ROWS)]
        scores = scale * lax.dot_general(
            rows_of(emb, at)[...], block, (((1,), (1,)), ((), ())),
            preferred_element_type=jnp.float32,
        ) + bias
        sign = signs[kind]
        first = sign * (0.0625 + 0.0625 * jnp.tanh((0.5 * sign) * scores[:, :ROWS]))
        second = 0.0625 + 0.0625 * jnp.tanh(0.5 * scores[:, ROWS:])
        slope = jnp.concatenate([first, second], axis=1).astype(jnp.bfloat16)
        here = rows_of(grad, at)
        here[...] += jnp.dot(slope, block, preferred_element_type=jnp.float32)
        return carry

    lax.fori_loop(0, 8, item, 0)

    def finish(slot, carry):
        unit = rows_of(raw, slot)[...]
        slope = scale * rows_of(grad, slot)[...]
        inner = jnp.sum(unit * slope, axis=1, keepdims=True)
        rows_of(raw_grad, slot)[...] = (
            (slope - unit * inner) * rows_of(inv, slot)[...]
        ).astype(jnp.bfloat16)
        return carry

    lax.fori_loop(0, 4, finish, 0)

    @pl.when(core == 1)
    def _():
        finish(4, 0)

    SIDE = HALF // 2

    def cols_of(j):
        return pl.ds(STARTS[j], WIDTHS[j])

    def wide_of(j):
        return pl.ds(STARTS[j] + 128 * j, WIDTHS[j] + 128)

    def main_of(j):
        return pl.ds(STARTS[j] + 128 * j, WIDTHS[j])

    def rest_of(j):
        return pl.ds(STARTS[j] + 128 * j + WIDTHS[j], 128)

    def y_copies(j):
        cols = cols_of(j)
        return (
            remote(y_out.at[pl.ds(0, SIDE), cols], y_in.at[pl.ds(0, SIDE), cols],
                   y_send.at[j, 0], y_recv.at[j, 0], near),
            remote(y_out.at[pl.ds(SIDE, SIDE), cols], y_in.at[pl.ds(SIDE, SIDE), cols],
                   y_send.at[j, 1], y_recv.at[j, 1], far),
        )

    for j in range(PARTS):
        cols = cols_of(j)
        y_out[:, cols] = jnp.dot(
            feats_t[pl.ds(other_half, HALF), :], raw_grad[:, cols], preferred_element_type=jnp.float32
        ).astype(jnp.bfloat16)
        for copy in y_copies(j):
            copy.start()
    for j in range(PARTS):
        cols = cols_of(j)
        total[:, cols] = jnp.dot(
            feats_t[pl.ds(own_half, HALF), :], raw_grad[:, cols], preferred_element_type=jnp.float32
        )

    def x_copy(j, k):
        cols = cols_of(j)
        return remote(x_out.at[k - 1, :, cols], x_in.at[k - 1, :, cols],
                      x_send.at[j, k - 1], x_recv.at[j, k - 1], x_peers[k - 1])

    def z_copy(j, k):
        cols = wide_of(j)
        return remote(z_out.at[k - 1, :, cols], z_in.at[k - 1, :, cols],
                      z_send.at[j, k - 1], z_recv.at[j, k - 1], z_peers[k - 1])

    def y2_copy(j):
        cols = wide_of(j)
        return remote(z_sum.at[:, cols], y2_in.at[:, cols], y2_send.at[j], y2_recv.at[j], across)

    def zag_copy(j, k):
        cols = wide_of(j)
        return remote(final.at[:, cols], z_all.at[k - 1, :, cols],
                      zag_send.at[j, k - 1], zag_recv.at[j, k - 1], z_peers[k - 1])

    def x_rows(at):
        return pl.ds(pl.multiple_of(at * XROWS, 16), XROWS)

    def xag_copy(j, k, at):
        rows, cols = x_rows(at), cols_of(j)
        return remote(mine.at[rows, cols], mine.at[rows, cols],
                      xag_send.at[j, k - 1], xag_recv.at[j, k - 1], x_peers[k - 1])

    def core_copy(j):
        cols = cols_of(j)
        return remote(mine.at[:, cols], other.at[:, cols], core_send.at[j], core_recv.at[j], sibling)

    def stage_a(j):
        cols = cols_of(j)
        for copy in y_copies(j):
            copy.wait_recv()
        for k in range(1, 4):
            rows = x_rows(lax.rem(x + k, 4))
            x_out[k - 1, :, cols] = (
                total[rows, cols] + y_in[rows, cols].astype(jnp.float32)
            ).astype(jnp.bfloat16)
            x_copy(j, k).start()
        x_sum[:, cols] = total[x_rows(x), cols] + y_in[x_rows(x), cols].astype(jnp.float32)

    def extra_cols(j, at):
        block = lax.div(at * (WIDTHS[j] // 128), 8)
        return pl.ds(pl.multiple_of(STARTS[j] + block * 128, 128), 128)

    def piece_rows(at):
        return pl.ds(pl.multiple_of(at * PIECE, PIECE), PIECE)

    def stage_b(j):
        cols = cols_of(j)
        for k in range(1, 4):
            x_copy(j, k).wait_recv()
        x_sum[:, cols] = (
            x_sum[:, cols] + x_in[0, :, cols].astype(jnp.float32)
        ) + (x_in[1, :, cols].astype(jnp.float32) + x_in[2, :, cols].astype(jnp.float32))
        for k in range(1, 8):
            at = lax.rem(z + k, 8)
            z_out[k - 1, :, main_of(j)] = x_sum[piece_rows(at), cols].astype(jnp.bfloat16)
            z_out[k - 1, :, rest_of(j)] = x_sum[8 * PIECE :, extra_cols(j, at)].astype(jnp.bfloat16)
            z_copy(j, k).start()
        z_sum[:, main_of(j)] = x_sum[piece_rows(z), cols]
        z_sum[:, rest_of(j)] = x_sum[8 * PIECE :, extra_cols(j, z)]

    def stage_c(j):
        cols = wide_of(j)
        for k in range(1, 8):
            z_copy(j, k).wait_recv()
        acc = z_sum[:, cols]
        for k in range(1, 8):
            acc = acc + z_in[k - 1, :, cols].astype(jnp.float32)
        z_sum[:, cols] = acc
        y2_copy(j).start()

    def place(j, at, piece):
        rows = pl.ds(pl.multiple_of(x * XROWS + at * PIECE, PIECE), PIECE)
        mine[rows, cols_of(j)] = piece[:, : WIDTHS[j]]
        tail = pl.ds(pl.multiple_of(x * XROWS + 8 * PIECE, PIECE), PIECE)
        blocks = WIDTHS[j] // 128
        for n in range(blocks):
            @pl.when(at == -(-8 * n // blocks))
            def _():
                mine[tail, pl.ds(STARTS[j] + n * 128, 128)] = piece[:, WIDTHS[j] :]

    def stage_d(j):
        cols = wide_of(j)
        y2_copy(j).wait_recv()
        final[:, cols] = (z_sum[:, cols] + y2_in[:, cols]).astype(jnp.bfloat16)
        for k in range(1, 8):
            zag_copy(j, k).start()
        place(j, z, final[:, cols])

    def stage_e(j):
        for k in range(1, 8):
            zag_copy(j, k).wait_recv()
            place(j, lax.rem(z + 8 - k, 8), z_all[k - 1, :, wide_of(j)])
        for k in range(1, 4):
            xag_copy(j, k, x).start()

    def stage_f(j):
        for k in range(1, 4):
            xag_copy(j, k, lax.rem(x + 4 - k, 4)).wait_recv()
        core_copy(j).start()

    def out_copies(j, first, second):
        cols = cols_of(j)
        return (
            pltpu.make_async_copy(mine.at[:, cols], first.at[:, cols], out_sem.at[j, 0]),
            pltpu.make_async_copy(other.at[:, cols], second.at[:, cols], out_sem.at[j, 1]),
        )

    def stage_g(j):
        core_copy(j).wait_recv()

        @pl.when(core == 0)
        def _():
            for copy in out_copies(j, image_out, text_out):
                copy.start()

        @pl.when(core == 1)
        def _():
            for copy in out_copies(j, text_out, image_out):
                copy.start()

    stages = (stage_a, stage_b, stage_c, stage_d, stage_e, stage_f, stage_g)
    for turn_at in range(len(stages) + PARTS - 1):
        for j in range(PARTS):
            if 0 <= turn_at - j < len(stages):
                stages[turn_at - j](j)

    for copy in head_copies(image_head_ref):
        copy.wait_send()
    for n in range(2):
        for k in range(1, 4):
            share_copy(n, k).wait_send()

    for which in range(2):
        feat_copy(image_ref, 0, which, sibling).wait_send()
    for n in range(BITS):
        bit_copy(text_ref, 0, n, 2, across).wait_send()

    @pl.when(core == 1)
    def _():
        for n in range(BITS):
            bit_copy(feats, 2, n, 4, across).wait_send()
        emb_copy(4).wait_send()

    @pl.when(leaves + turns == 1)
    def _():
        for n in range(BITS):
            relay_on(n, 2, across).wait_send()

    for slot in range(4):
        emb_copy(slot).wait_send()
    for j in range(PARTS):
        for copy in y_copies(j):
            copy.wait_send()
        for k in range(1, 4):
            x_copy(j, k).wait_send()
            xag_copy(j, k, x).wait_send()
        for k in range(1, 8):
            z_copy(j, k).wait_send()
            zag_copy(j, k).wait_send()
        y2_copy(j).wait_send()
        core_copy(j).wait_send()
        for copy in out_copies(j, image_out, text_out):
            copy.wait()


def widen(image_ref, text_ref, image_out, text_out):
    image_out[...] = image_ref[...].astype(jnp.float32)
    text_out[...] = text_ref[...].astype(jnp.float32)


def on_device(
    image_features, text_features, image_head, text_head, pair_index, logit_scale, logit_bias
):
    hbm = pl.BlockSpec(memory_space=pl.ANY)
    smem = pl.BlockSpec(memory_space=pltpu.SMEM)
    bf16, f32 = jnp.bfloat16, jnp.float32
    vmem = pltpu.VMEM
    dma = pltpu.SemaphoreType.DMA
    image_half, text_half = pl.pallas_call(
        kernel,
        out_shape=(
            jax.ShapeDtypeStruct((HALF, E), bf16),
            jax.ShapeDtypeStruct((HALF, E), bf16),
        ),
        in_specs=[hbm, hbm, hbm, hbm, hbm, smem, smem],
        out_specs=(hbm, hbm),
        scratch_shapes=[
            vmem((SLOTS * ROWS, E), bf16),
            vmem((E, SLOTS * ROWS), bf16),
            vmem((E, E), bf16),
            vmem((SLOTS * ROWS, E), f32),
            vmem((SLOTS * ROWS, 1), f32),
            vmem((SLOTS * ROWS, E), bf16),
            vmem((SLOTS * ROWS, E), bf16),
            vmem((SLOTS * ROWS, E), f32),
            vmem((SLOTS * ROWS, E), bf16),
            vmem((ROWS, E), bf16),
            vmem((2, 1, ROWS), jnp.int32),
            vmem((3, ROWS, ROWS), f32),
            vmem((HALF, E), bf16),
            vmem((HALF, E), bf16),
            vmem((HALF, E), f32),
            vmem((3, XROWS, E), bf16),
            vmem((3, XROWS, E), bf16),
            vmem((XROWS, E), f32),
            vmem((7, PIECE, PWIDE), bf16),
            vmem((7, PIECE, PWIDE), bf16),
            vmem((PIECE, PWIDE), f32),
            vmem((PIECE, PWIDE), f32),
            vmem((PIECE, PWIDE), bf16),
            vmem((7, PIECE, PWIDE), bf16),
            vmem((HALF, E), bf16),
            vmem((HALF, E), bf16),
            dma((2,)),
            dma((SLOTS,)),
            dma((2, BITS)),
            dma((3, BITS)),
            dma((BITS,)),
            dma((BITS,)),
            dma((9,)),
            dma((10,)),
            dma((2,)),
            dma,
            dma((SLOTS,)),
            dma((SLOTS,)),
            dma((PARTS, 2)),
            dma((PARTS, 2)),
            dma((PARTS, 3)),
            dma((PARTS, 3)),
            dma((PARTS, 7)),
            dma((PARTS, 7)),
            dma((PARTS,)),
            dma((PARTS,)),
            dma((PARTS, 7)),
            dma((PARTS, 7)),
            dma((PARTS, 3)),
            dma((PARTS, 3)),
            dma((PARTS,)),
            dma((PARTS,)),
            dma((PARTS, 2)),
        ],
        compiler_params=pltpu.CompilerParams(
            collective_id=0, has_side_effects=True, vmem_limit_bytes=60 * 2**20
        ),
        cost_estimate=pl.CostEstimate(
            flops=12 * 10**9, bytes_accessed=12 * 10**6, transcendentals=10**6
        ),
    )(image_features, text_features, image_head, text_head, pair_index, logit_scale, logit_bias)
    block = pl.BlockSpec((HALF // WIDEN, E), lambda n: (n, 0))
    return pl.pallas_call(
        widen,
        grid=(WIDEN,),
        out_shape=(
            jax.ShapeDtypeStruct((HALF, E), f32),
            jax.ShapeDtypeStruct((HALF, E), f32),
        ),
        in_specs=[block, block],
        out_specs=(block, block),
        compiler_params=pltpu.CompilerParams(vmem_limit_bytes=60 * 2**20),
        cost_estimate=pl.CostEstimate(flops=2 * HALF * E, bytes_accessed=12 * HALF * E, transcendentals=0),
    )(image_half, text_half)


def solution(mesh):
    placed = (
        P(("blk", "fsdp"), None),
        P(("blk", "fsdp"), None),
        P("fsdp", None),
        P("fsdp", None),
        P(("blk", "fsdp"), None),
        P(),
        P(),
    )
    return jax.shard_map(
        on_device,
        mesh=mesh,
        in_specs=placed,
        out_specs=(P("fsdp", None), P("fsdp", None)),
        check_vma=False,
    )
```

```python
import jax
import jax.numpy as jnp
from jax import lax
from jax.experimental import pallas as pl
from jax.experimental.pallas import tpu as pltpu
from jax.sharding import PartitionSpec as P

STEPS = 8
MESH = pl.DeviceIdType.MESH
ROWS = 256
E = 1152
HALF = E // 2
SLOTS = 5
EARLY = 512
WIDEN = 2
WIDTHS = (384, 384, 384)
PARTS = len(WIDTHS)
STARTS = tuple(sum(WIDTHS[:n]) for n in range(PARTS))
BITS = 4
RELAY = 0
BIT = ROWS // BITS
DIRECT = 192
SHARE = (HALF - DIRECT) // 4
SHARE_FAR = 64
SHARE_NEAR = SHARE - SHARE_FAR
XROWS = HALF // 4
PIECE = 16
PWIDE = E + 128 * PARTS


def device_of(x, yh, f, z, core):
    return (((yh * 4 + x) * 8 + z) * 2 + core, f)


def shifted(index, by):
    other = lax.rem(index + (by + 256), 256)
    return (lax.div(other, 2), lax.rem(other, 2))


def is_equal(n, k):
    gap = n - k
    return 1 - lax.div(gap * gap + 99, 100)


def kernel(
    image_ref,
    text_ref,
    image_head_ref,
    text_head_ref,
    pair_ref,
    scale_ref,
    bias_ref,
    image_out,
    text_out,
    feats,
    feats_t,
    head,
    raw,
    inv,
    emb,
    emb_other,
    grad,
    raw_grad,
    relay,
    pairs,
    signs,
    y_out,
    y_in,
    total,
    x_out,
    x_in,
    x_sum,
    z_out,
    z_in,
    z_sum,
    y2_in,
    final,
    z_all,
    mine,
    other,
    feat_send,
    feat_recv,
    bit_send,
    bit_recv,
    relay_send,
    relay_recv,
    head_send,
    head_recv,
    pair_send,
    pair_recv,
    emb_send,
    emb_recv,
    y_send,
    y_recv,
    x_send,
    x_recv,
    z_send,
    z_recv,
    y2_send,
    y2_recv,
    zag_send,
    zag_recv,
    xag_send,
    xag_recv,
    core_send,
    core_recv,
    out_sem,
):
    blk = lax.axis_index("blk")
    f = lax.axis_index("fsdp")
    core = lax.rem(blk, 2)
    z = lax.rem(lax.div(blk, 2), 8)
    x = lax.rem(lax.div(blk, 16), 4)
    yh = lax.div(blk, 64)
    index = blk * 2 + f
    sibling = device_of(x, yh, f, z, 1 - core)
    near = device_of(x, yh, 1 - f, z, core)
    far = device_of(x, 1 - yh, 1 - f, z, core)
    across = device_of(x, 1 - yh, f, z, core)
    x_peers = [device_of(lax.rem(x + k, 4), yh, f, z, core) for k in range(1, 4)]
    z_peers = [device_of(x, yh, f, lax.rem(z + k, 8), core) for k in range(1, 8)]
    step = 3 - 2 * lax.rem(core + f, 2)

    barrier = pltpu.get_barrier_semaphore()

    def hello(device):
        pl.semaphore_signal(barrier, inc=1, device_id=device, device_id_type=MESH)

    for device in [sibling, near, far, across] + x_peers + z_peers:
        hello(device)

    @pl.when(core == 0)
    def _():
        hello(shifted(index, 1))
        hello(shifted(index, 3))

    z_last = lax.div(z, 7)
    z_first = (1 - lax.div(z + 6, 7)) * core
    leaves = z_last * (1 - core)
    turns = z_last * lax.div(x, 3) * core * RELAY
    starts = z_first * (1 - lax.div(x + 2, 3)) * RELAY
    ahead = shifted(index, 32)

    @pl.when(core == 1)
    def _():
        hello(shifted(index, -4))

        @pl.when(z_first == 0)
        def _():
            hello(shifted(index, -6))

        @pl.when(z_first == 1)
        def _():
            hello(device_of(x, yh, f, 7, 0))

    @pl.when(starts == 1)
    def _():
        hello(device_of(3, yh, f, 7, 1))

    @pl.when(leaves == 1)
    def _():
        hello(shifted(index, -32))

    def rows_of(ref, slot):
        start = slot * ROWS
        if not isinstance(slot, int):
            start = pl.multiple_of(start, ROWS)
        return ref.at[pl.ds(start, ROWS)]

    def remote(src, dst, send, recv, device):
        return pltpu.make_async_remote_copy(
            src_ref=src, dst_ref=dst, send_sem=send, recv_sem=recv,
            device_id=device, device_id_type=MESH,
        )

    def feat_copy(src, slot, which, device):
        return remote(src, rows_of(feats, slot), feat_send.at[which], feat_recv.at[slot], device)

    own_half = pl.multiple_of(f * HALF, 16)
    own_pair = pltpu.make_async_copy(pair_ref, pairs.at[0], pair_send.at[0])
    own_pair.start()

    @pl.when(core == 0)
    def _():
        pltpu.make_async_copy(image_ref, rows_of(feats, 0), feat_recv.at[0]).start()
        pltpu.make_async_copy(image_head_ref, head.at[pl.ds(own_half, HALF)], head_recv.at[0]).start()

    @pl.when(core == 1)
    def _():
        pltpu.make_async_copy(text_ref, rows_of(feats, 0), feat_recv.at[0]).start()
        pltpu.make_async_copy(text_head_ref, head.at[pl.ds(own_half, HALF)], head_recv.at[0]).start()

    pl.semaphore_wait(barrier, 16 + leaves + turns)

    def half_rows(half, start, size):
        return pl.ds(pl.multiple_of(half * HALF + start, 16), size)

    def head_copy(src, n, start, size, device):
        return remote(src.at[pl.ds(pl.multiple_of(start, 16), size)], head.at[half_rows(f, start, size)],
                      head_send.at[n], head_recv.at[n + 1], device)

    def head_copies(src):
        return (
            head_copy(src, 1, DIRECT + SHARE * x, SHARE_FAR, far),
            head_copy(src, 2, DIRECT + SHARE * x + SHARE_FAR, SHARE_NEAR, near),
            head_copy(src, 0, 0, DIRECT, far),
        )

    def share_rows(owner, n):
        start = DIRECT + SHARE * owner + n * SHARE_FAR
        return half_rows(1 - f, start, (SHARE_FAR, SHARE_NEAR)[n])

    def share_copy(n, k):
        rows = share_rows(x, n)
        return remote(head.at[rows], head.at[rows], head_send.at[3 + 3 * n + k - 1],
                      head_recv.at[4 + 3 * n + k - 1], x_peers[k - 1])

    pair_copy = remote(pair_ref, pairs.at[1], pair_send.at[1], pair_recv, sibling)

    def bit_copy(src, src_slot, n, slot, device):
        start = slot * ROWS + n * BIT
        return remote(src.at[pl.ds(src_slot * ROWS + n * BIT, BIT)], feats.at[pl.ds(start, BIT)],
                      bit_send.at[slot // 4, n], bit_recv.at[slot - 2, n], device)

    def relay_in(src, n, device):
        rows = pl.ds(n * BIT, BIT)
        return remote(src.at[rows], relay.at[rows], bit_send.at[0, n], relay_recv.at[n], device)

    def relay_on(n, slot, device):
        return remote(relay.at[pl.ds(n * BIT, BIT)], feats.at[pl.ds(slot * ROWS + n * BIT, BIT)],
                      relay_send.at[n], bit_recv.at[slot - 2, n], device)

    def bit_wait(slot, n):
        bit_copy(feats, slot, n, slot, across).wait_recv()

    @pl.when(core == 0)
    def _():


        for copy in head_copies(image_head_ref):
            copy.start()

        @pl.when(leaves == 0)
        def _():
            for n in range(BITS):
                bit_copy(text_ref, 0, n, 3, shifted(index, 6)).start()

        @pl.when(leaves == 1)
        def _():
            for n in range(BITS):
                relay_in(text_ref, n, ahead).start()

        feat_copy(image_ref, step, 0, shifted(index, -step)).start()
        feat_copy(text_ref, 1, 1, sibling).start()

    @pl.when(core == 1)
    def _():

        for copy in head_copies(text_head_ref):
            copy.start()

        @pl.when(turns == 0)
        def _():
            for n in range(BITS):
                bit_copy(text_ref, 0, n, 2, shifted(index, 4)).start()

        @pl.when(turns == 1)
        def _():
            for n in range(BITS):
                relay_in(text_ref, n, across).start()

        feat_copy(image_ref, step, 0, shifted(index, -step)).start()
        feat_copy(image_ref, 2, 1, sibling).start()

    pair_copy.start()

    grad[...] = jnp.zeros_like(grad)

    @pl.when(core == 0)
    def _():
        rows_of(feats, 4)[...] = jnp.zeros((ROWS, E), jnp.bfloat16)
        rows_of(raw_grad, 4)[...] = jnp.zeros((ROWS, E), jnp.bfloat16)

    own_pair.wait()
    pair_copy.wait()
    signs[2] = jnp.ones((ROWS, ROWS), jnp.float32)
    for which in range(2):
        hit = lax.broadcasted_iota(jnp.int32, (ROWS, ROWS), 0) == pairs[which]
        sign = jnp.where(hit, -1.0, 1.0).astype(jnp.float32)

        @pl.when(core == 0)
        def _():
            signs[which] = sign.T

        @pl.when(core == 1)
        def _():
            signs[1 - which] = sign

    def feat_wait(slot):
        pltpu.make_async_copy(rows_of(feats, slot), rows_of(feats, slot), feat_recv.at[slot]).wait()

    def turn(slot):
        feats_t[:, slot * ROWS : (slot + 1) * ROWS] = rows_of(feats, slot)[...].T

    def head_wait(rows, sem):
        pltpu.make_async_copy(head.at[rows], head.at[rows], head_recv.at[sem]).wait()

    other_half = pl.multiple_of((1 - f) * HALF, 16)

    for n in range(2):
        head_wait(share_rows(x, n), 2 + n)
        for k in range(1, 4):
            share_copy(n, k).start()

    for n in range(BITS):
        @pl.when(leaves == 1)
        def _():
            relay_in(text_ref, n, ahead).wait_recv()
            relay_on(n, 3, device_of(x, yh, f, 0, 1)).start()

        @pl.when(turns == 1)
        def _():
            relay_in(text_ref, n, across).wait_recv()
            relay_on(n, 2, device_of(0, yh, f, 0, 1)).start()

        @pl.when(core == 1)
        def _():
            bit_wait(2, n)
            bit_copy(feats, 2, n, 4, shifted(index, 4)).start()

    @pl.when(core == 0)
    def _():
        feat_wait(2)

    for slot in (0, 1):
        feat_wait(slot)

    head_wait(pl.ds(own_half, HALF), 0)
    early = pl.ds(pl.multiple_of(f * (E - EARLY), 128), EARLY)
    late = pl.ds(pl.multiple_of((1 - f) * EARLY, 128), E - EARLY)

    def begin(slot, carry):
        rows_of(raw, slot)[...] = jnp.dot(
            rows_of(feats, slot)[:, early], head[early, :], preferred_element_type=jnp.float32
        )
        return carry

    lax.fori_loop(0, 3, begin, 0)
    for slot in (0, 1, 2):
        turn(slot)

    head_wait(half_rows(1 - f, 0, DIRECT), 1)
    for n in range(2):
        for k in range(1, 4):
            head_wait(share_rows(lax.rem(x + 4 - k, 4), n), 4 + 3 * n + k - 1)

    def emb_copy(slot):
        return remote(rows_of(emb, slot), rows_of(emb_other, slot),
                      emb_send.at[slot], emb_recv.at[slot], sibling)

    def embed(slot):
        product = rows_of(raw, slot)[...] + jnp.dot(
            rows_of(feats, slot)[:, late], head[late, :], preferred_element_type=jnp.float32
        )
        inverse = lax.rsqrt(jnp.sum(product * product, axis=1, keepdims=True) + 1e-06)
        unit = product * inverse
        rows_of(raw, slot)[...] = unit
        rows_of(inv, slot)[...] = inverse
        rows_of(emb, slot)[...] = unit.astype(jnp.bfloat16)
        emb_copy(slot).start()

    def embed_step(slot, carry):
        @pl.when((slot == 3) & (core == 0))
        def _():
            feat_wait(3)

        @pl.when((slot == 3) & (core == 1))
        def _():
            for n in range(BITS):
                bit_wait(3, n)

        @pl.when(slot == 3)
        def _():
            begin(3, 0)

        embed(slot)
        return carry

    lax.fori_loop(0, 4, embed_step, 0)

    @pl.when(core == 1)
    def _():
        for n in range(BITS):
            bit_wait(4, n)
        begin(4, 0)
        embed(4)

    turn(3)
    turn(4)

    for slot in range(4):
        @pl.when(core == 0)
        def _():
            emb_copy(slot).wait_recv()

        @pl.when(core == 1)
        def _():
            emb_copy(slot).wait_recv()

    @pl.when(core == 0)
    def _():
        emb_copy(4).wait_recv()

    scale = scale_ref[0]
    bias = bias_ref[0]

    def item(n, carry):
        at0 = lax.div(n, 2)
        at1 = lax.div(n + 1, 2)
        col0 = 1 - lax.div(at0, 2) + 2 * lax.rem(n, 2)
        col1 = 2 * lax.rem(n + 1, 2)
        at = at0 + core * (at1 - at0)
        col = col0 + core * (col1 - col0)
        kind = 2 - (
            is_equal(n, 0) * (2 - core) + is_equal(n, 4) * (1 - core) + is_equal(n, 1) * 2 * core
        )
        block = emb_other[pl.ds(pl.multiple_of(col * ROWS, ROWS), 2 * ROWS)]
        scores = scale * lax.dot_general(
            rows_of(emb, at)[...], block, (((1,), (1,)), ((), ())),
            preferred_element_type=jnp.float32,
        ) + bias
        sign = signs[kind]
        first = sign * (0.0625 + 0.0625 * jnp.tanh((0.5 * sign) * scores[:, :ROWS]))
        second = 0.0625 + 0.0625 * jnp.tanh(0.5 * scores[:, ROWS:])
        slope = jnp.concatenate([first, second], axis=1).astype(jnp.bfloat16)
        here = rows_of(grad, at)
        here[...] += jnp.dot(slope, block, preferred_element_type=jnp.float32)
        return carry

    lax.fori_loop(0, 8, item, 0)

    def finish(slot, carry):
        unit = rows_of(raw, slot)[...]
        slope = scale * rows_of(grad, slot)[...]
        inner = jnp.sum(unit * slope, axis=1, keepdims=True)
        rows_of(raw_grad, slot)[...] = (
            (slope - unit * inner) * rows_of(inv, slot)[...]
        ).astype(jnp.bfloat16)
        return carry

    lax.fori_loop(0, 4, finish, 0)

    @pl.when(core == 1)
    def _():
        finish(4, 0)

    SIDE = HALF // 2

    def cols_of(j):
        return pl.ds(STARTS[j], WIDTHS[j])

    def wide_of(j):
        return pl.ds(STARTS[j] + 128 * j, WIDTHS[j] + 128)

    def main_of(j):
        return pl.ds(STARTS[j] + 128 * j, WIDTHS[j])

    def rest_of(j):
        return pl.ds(STARTS[j] + 128 * j + WIDTHS[j], 128)

    def y_copies(j):
        cols = cols_of(j)
        return (
            remote(y_out.at[pl.ds(0, SIDE), cols], y_in.at[pl.ds(0, SIDE), cols],
                   y_send.at[j, 0], y_recv.at[j, 0], near),
            remote(y_out.at[pl.ds(SIDE, SIDE), cols], y_in.at[pl.ds(SIDE, SIDE), cols],
                   y_send.at[j, 1], y_recv.at[j, 1], far),
        )

    for j in range(PARTS):
        cols = cols_of(j)
        y_out[:, cols] = jnp.dot(
            feats_t[pl.ds(other_half, HALF), :], raw_grad[:, cols], preferred_element_type=jnp.float32
        ).astype(jnp.bfloat16)
        for copy in y_copies(j):
            copy.start()
    for j in range(PARTS):
        cols = cols_of(j)
        total[:, cols] = jnp.dot(
            feats_t[pl.ds(own_half, HALF), :], raw_grad[:, cols], preferred_element_type=jnp.float32
        )

    def x_copy(j, k):
        cols = cols_of(j)
        return remote(x_out.at[k - 1, :, cols], x_in.at[k - 1, :, cols],
                      x_send.at[j, k - 1], x_recv.at[j, k - 1], x_peers[k - 1])

    def z_copy(j, k):
        cols = wide_of(j)
        return remote(z_out.at[k - 1, :, cols], z_in.at[k - 1, :, cols],
                      z_send.at[j, k - 1], z_recv.at[j, k - 1], z_peers[k - 1])

    def y2_copy(j):
        cols = wide_of(j)
        return remote(z_sum.at[:, cols], y2_in.at[:, cols], y2_send.at[j], y2_recv.at[j], across)

    def zag_copy(j, k):
        cols = wide_of(j)
        return remote(final.at[:, cols], z_all.at[k - 1, :, cols],
                      zag_send.at[j, k - 1], zag_recv.at[j, k - 1], z_peers[k - 1])

    def x_rows(at):
        return pl.ds(pl.multiple_of(at * XROWS, 16), XROWS)

    def xag_copy(j, k, at):
        rows, cols = x_rows(at), cols_of(j)
        return remote(mine.at[rows, cols], mine.at[rows, cols],
                      xag_send.at[j, k - 1], xag_recv.at[j, k - 1], x_peers[k - 1])

    def core_copy(j):
        cols = cols_of(j)
        return remote(mine.at[:, cols], other.at[:, cols], core_send.at[j], core_recv.at[j], sibling)

    def stage_a(j):
        cols = cols_of(j)
        for copy in y_copies(j):
            copy.wait_recv()
        for k in range(1, 4):
            rows = x_rows(lax.rem(x + k, 4))
            x_out[k - 1, :, cols] = (
                total[rows, cols] + y_in[rows, cols].astype(jnp.float32)
            ).astype(jnp.bfloat16)
            x_copy(j, k).start()
        x_sum[:, cols] = total[x_rows(x), cols] + y_in[x_rows(x), cols].astype(jnp.float32)

    def extra_cols(j, at):
        block = lax.div(at * (WIDTHS[j] // 128), 8)
        return pl.ds(pl.multiple_of(STARTS[j] + block * 128, 128), 128)

    def piece_rows(at):
        return pl.ds(pl.multiple_of(at * PIECE, PIECE), PIECE)

    def stage_b(j):
        cols = cols_of(j)
        for k in range(1, 4):
            x_copy(j, k).wait_recv()
        x_sum[:, cols] = (
            x_sum[:, cols] + x_in[0, :, cols].astype(jnp.float32)
        ) + (x_in[1, :, cols].astype(jnp.float32) + x_in[2, :, cols].astype(jnp.float32))
        for k in range(1, 8):
            at = lax.rem(z + k, 8)
            z_out[k - 1, :, main_of(j)] = x_sum[piece_rows(at), cols].astype(jnp.bfloat16)
            z_out[k - 1, :, rest_of(j)] = x_sum[8 * PIECE :, extra_cols(j, at)].astype(jnp.bfloat16)
            z_copy(j, k).start()
        z_sum[:, main_of(j)] = x_sum[piece_rows(z), cols]
        z_sum[:, rest_of(j)] = x_sum[8 * PIECE :, extra_cols(j, z)]

    def stage_c(j):
        cols = wide_of(j)
        for k in range(1, 8):
            z_copy(j, k).wait_recv()
        acc = z_sum[:, cols]
        for k in range(1, 8):
            acc = acc + z_in[k - 1, :, cols].astype(jnp.float32)
        z_sum[:, cols] = acc
        y2_copy(j).start()

    def place(j, at, piece):
        rows = pl.ds(pl.multiple_of(x * XROWS + at * PIECE, PIECE), PIECE)
        mine[rows, cols_of(j)] = piece[:, : WIDTHS[j]]
        tail = pl.ds(pl.multiple_of(x * XROWS + 8 * PIECE, PIECE), PIECE)
        blocks = WIDTHS[j] // 128
        for n in range(blocks):
            @pl.when(at == -(-8 * n // blocks))
            def _():
                mine[tail, pl.ds(STARTS[j] + n * 128, 128)] = piece[:, WIDTHS[j] :]

    def stage_d(j):
        cols = wide_of(j)
        y2_copy(j).wait_recv()
        final[:, cols] = (z_sum[:, cols] + y2_in[:, cols]).astype(jnp.bfloat16)
        for k in range(1, 8):
            zag_copy(j, k).start()
        place(j, z, final[:, cols])

    def stage_e(j):
        for k in range(1, 8):
            zag_copy(j, k).wait_recv()
            place(j, lax.rem(z + 8 - k, 8), z_all[k - 1, :, wide_of(j)])
        for k in range(1, 4):
            xag_copy(j, k, x).start()

    def stage_f(j):
        for k in range(1, 4):
            xag_copy(j, k, lax.rem(x + 4 - k, 4)).wait_recv()
        core_copy(j).start()

    def out_copies(j, first, second):
        cols = cols_of(j)
        return (
            pltpu.make_async_copy(mine.at[:, cols], first.at[:, cols], out_sem.at[j, 0]),
            pltpu.make_async_copy(other.at[:, cols], second.at[:, cols], out_sem.at[j, 1]),
        )

    def stage_g(j):
        core_copy(j).wait_recv()

        @pl.when(core == 0)
        def _():
            for copy in out_copies(j, image_out, text_out):
                copy.start()

        @pl.when(core == 1)
        def _():
            for copy in out_copies(j, text_out, image_out):
                copy.start()

    stages = (stage_a, stage_b, stage_c, stage_d, stage_e, stage_f, stage_g)
    for turn_at in range(len(stages) + PARTS - 1):
        for j in range(PARTS):
            if 0 <= turn_at - j < len(stages):
                stages[turn_at - j](j)

    for copy in head_copies(image_head_ref):
        copy.wait_send()
    for n in range(2):
        for k in range(1, 4):
            share_copy(n, k).wait_send()

    for which in range(2):
        feat_copy(image_ref, 0, which, sibling).wait_send()
    for n in range(BITS):
        bit_copy(text_ref, 0, n, 2, across).wait_send()

    @pl.when(core == 1)
    def _():
        for n in range(BITS):
            bit_copy(feats, 2, n, 4, across).wait_send()
        emb_copy(4).wait_send()

    @pl.when(leaves + turns == 1)
    def _():
        for n in range(BITS):
            relay_on(n, 2, across).wait_send()

    for slot in range(4):
        emb_copy(slot).wait_send()
    for j in range(PARTS):
        for copy in y_copies(j):
            copy.wait_send()
        for k in range(1, 4):
            x_copy(j, k).wait_send()
            xag_copy(j, k, x).wait_send()
        for k in range(1, 8):
            z_copy(j, k).wait_send()
            zag_copy(j, k).wait_send()
        y2_copy(j).wait_send()
        core_copy(j).wait_send()
        for copy in out_copies(j, image_out, text_out):
            copy.wait()


def widen(image_ref, text_ref, image_out, text_out):
    image_out[...] = image_ref[...].astype(jnp.float32)
    text_out[...] = text_ref[...].astype(jnp.float32)


def on_device(
    image_features, text_features, image_head, text_head, pair_index, logit_scale, logit_bias
):
    hbm = pl.BlockSpec(memory_space=pl.ANY)
    smem = pl.BlockSpec(memory_space=pltpu.SMEM)
    bf16, f32 = jnp.bfloat16, jnp.float32
    vmem = pltpu.VMEM
    dma = pltpu.SemaphoreType.DMA
    image_half, text_half = pl.pallas_call(
        kernel,
        out_shape=(
            jax.ShapeDtypeStruct((HALF, E), bf16),
            jax.ShapeDtypeStruct((HALF, E), bf16),
        ),
        in_specs=[hbm, hbm, hbm, hbm, hbm, smem, smem],
        out_specs=(hbm, hbm),
        scratch_shapes=[
            vmem((SLOTS * ROWS, E), bf16),
            vmem((E, SLOTS * ROWS), bf16),
            vmem((E, E), bf16),
            vmem((SLOTS * ROWS, E), f32),
            vmem((SLOTS * ROWS, 1), f32),
            vmem((SLOTS * ROWS, E), bf16),
            vmem((SLOTS * ROWS, E), bf16),
            vmem((SLOTS * ROWS, E), f32),
            vmem((SLOTS * ROWS, E), bf16),
            vmem((ROWS, E), bf16),
            vmem((2, 1, ROWS), jnp.int32),
            vmem((3, ROWS, ROWS), f32),
            vmem((HALF, E), bf16),
            vmem((HALF, E), bf16),
            vmem((HALF, E), f32),
            vmem((3, XROWS, E), bf16),
            vmem((3, XROWS, E), bf16),
            vmem((XROWS, E), f32),
            vmem((7, PIECE, PWIDE), bf16),
            vmem((7, PIECE, PWIDE), bf16),
            vmem((PIECE, PWIDE), f32),
            vmem((PIECE, PWIDE), f32),
            vmem((PIECE, PWIDE), bf16),
            vmem((7, PIECE, PWIDE), bf16),
            vmem((HALF, E), bf16),
            vmem((HALF, E), bf16),
            dma((2,)),
            dma((SLOTS,)),
            dma((2, BITS)),
            dma((3, BITS)),
            dma((BITS,)),
            dma((BITS,)),
            dma((9,)),
            dma((10,)),
            dma((2,)),
            dma,
            dma((SLOTS,)),
            dma((SLOTS,)),
            dma((PARTS, 2)),
            dma((PARTS, 2)),
            dma((PARTS, 3)),
            dma((PARTS, 3)),
            dma((PARTS, 7)),
            dma((PARTS, 7)),
            dma((PARTS,)),
            dma((PARTS,)),
            dma((PARTS, 7)),
            dma((PARTS, 7)),
            dma((PARTS, 3)),
            dma((PARTS, 3)),
            dma((PARTS,)),
            dma((PARTS,)),
            dma((PARTS, 2)),
        ],
        compiler_params=pltpu.CompilerParams(
            collective_id=0, has_side_effects=True, vmem_limit_bytes=60 * 2**20
        ),
        cost_estimate=pl.CostEstimate(
            flops=12 * 10**9, bytes_accessed=12 * 10**6, transcendentals=10**6
        ),
    )(image_features, text_features, image_head, text_head, pair_index, logit_scale, logit_bias)
    block = pl.BlockSpec((HALF // WIDEN, E), lambda n: (n, 0))
    return pl.pallas_call(
        widen,
        grid=(WIDEN,),
        out_shape=(
            jax.ShapeDtypeStruct((HALF, E), f32),
            jax.ShapeDtypeStruct((HALF, E), f32),
        ),
        in_specs=[block, block],
        out_specs=(block, block),
        compiler_params=pltpu.CompilerParams(vmem_limit_bytes=60 * 2**20),
        cost_estimate=pl.CostEstimate(flops=2 * HALF * E, bytes_accessed=12 * HALF * E, transcendentals=0),
    )(image_half, text_half)


def solution(mesh):
    placed = (
        P(("blk", "fsdp"), None),
        P(("blk", "fsdp"), None),
        P("fsdp", None),
        P("fsdp", None),
        P(("blk", "fsdp"), None),
        P(),
        P(),
    )
    return jax.shard_map(
        on_device,
        mesh=mesh,
        in_specs=placed,
        out_specs=(P("fsdp", None), P("fsdp", None)),
        check_vma=False,
    )
```

```python
import jax
import jax.numpy as jnp
from jax import lax
from jax.experimental import pallas as pl
from jax.experimental.pallas import tpu as pltpu
from jax.sharding import PartitionSpec as P

STEPS = 8
MESH = pl.DeviceIdType.MESH
ROWS = 256
E = 1152
HALF = E // 2
SLOTS = 5
EARLY = 512
WIDEN = 2
WIDTHS = (256, 512, 384)
PARTS = len(WIDTHS)
STARTS = tuple(sum(WIDTHS[:n]) for n in range(PARTS))
BITS = 4
RELAY = 0
BIT = ROWS // BITS
DIRECT = 192
SHARE = (HALF - DIRECT) // 4
SHARE_FAR = 64
SHARE_NEAR = SHARE - SHARE_FAR
XROWS = HALF // 4
PIECE = 16
PWIDE = E + 128 * PARTS


def device_of(x, yh, f, z, core):
    return (((yh * 4 + x) * 8 + z) * 2 + core, f)


def shifted(index, by):
    other = lax.rem(index + (by + 256), 256)
    return (lax.div(other, 2), lax.rem(other, 2))


def is_equal(n, k):
    gap = n - k
    return 1 - lax.div(gap * gap + 99, 100)


def kernel(
    image_ref,
    text_ref,
    image_head_ref,
    text_head_ref,
    pair_ref,
    scale_ref,
    bias_ref,
    image_out,
    text_out,
    feats,
    feats_t,
    head,
    raw,
    inv,
    emb,
    emb_other,
    grad,
    raw_grad,
    relay,
    pairs,
    signs,
    y_out,
    y_in,
    total,
    x_out,
    x_in,
    x_sum,
    z_out,
    z_in,
    z_sum,
    y2_in,
    final,
    z_all,
    mine,
    other,
    feat_send,
    feat_recv,
    bit_send,
    bit_recv,
    relay_send,
    relay_recv,
    head_send,
    head_recv,
    pair_send,
    pair_recv,
    emb_send,
    emb_recv,
    y_send,
    y_recv,
    x_send,
    x_recv,
    z_send,
    z_recv,
    y2_send,
    y2_recv,
    zag_send,
    zag_recv,
    xag_send,
    xag_recv,
    core_send,
    core_recv,
    out_sem,
):
    blk = lax.axis_index("blk")
    f = lax.axis_index("fsdp")
    core = lax.rem(blk, 2)
    z = lax.rem(lax.div(blk, 2), 8)
    x = lax.rem(lax.div(blk, 16), 4)
    yh = lax.div(blk, 64)
    index = blk * 2 + f
    sibling = device_of(x, yh, f, z, 1 - core)
    near = device_of(x, yh, 1 - f, z, core)
    far = device_of(x, 1 - yh, 1 - f, z, core)
    across = device_of(x, 1 - yh, f, z, core)
    x_peers = [device_of(lax.rem(x + k, 4), yh, f, z, core) for k in range(1, 4)]
    z_peers = [device_of(x, yh, f, lax.rem(z + k, 8), core) for k in range(1, 8)]
    step = 3 - 2 * lax.rem(core + f, 2)

    barrier = pltpu.get_barrier_semaphore()

    def hello(device):
        pl.semaphore_signal(barrier, inc=1, device_id=device, device_id_type=MESH)

    for device in [sibling, near, far, across] + x_peers + z_peers:
        hello(device)

    @pl.when(core == 0)
    def _():
        hello(shifted(index, 1))
        hello(shifted(index, 3))

    z_last = lax.div(z, 7)
    z_first = (1 - lax.div(z + 6, 7)) * core
    leaves = z_last * (1 - core)
    turns = z_last * lax.div(x, 3) * core * RELAY
    starts = z_first * (1 - lax.div(x + 2, 3)) * RELAY
    ahead = shifted(index, 32)

    @pl.when(core == 1)
    def _():
        hello(shifted(index, -4))

        @pl.when(z_first == 0)
        def _():
            hello(shifted(index, -6))

        @pl.when(z_first == 1)
        def _():
            hello(device_of(x, yh, f, 7, 0))

    @pl.when(starts == 1)
    def _():
        hello(device_of(3, yh, f, 7, 1))

    @pl.when(leaves == 1)
    def _():
        hello(shifted(index, -32))

    def rows_of(ref, slot):
        start = slot * ROWS
        if not isinstance(slot, int):
            start = pl.multiple_of(start, ROWS)
        return ref.at[pl.ds(start, ROWS)]

    def remote(src, dst, send, recv, device):
        return pltpu.make_async_remote_copy(
            src_ref=src, dst_ref=dst, send_sem=send, recv_sem=recv,
            device_id=device, device_id_type=MESH,
        )

    def feat_copy(src, slot, which, device):
        return remote(src, rows_of(feats, slot), feat_send.at[which], feat_recv.at[slot], device)

    own_half = pl.multiple_of(f * HALF, 16)
    own_pair = pltpu.make_async_copy(pair_ref, pairs.at[0], pair_send.at[0])
    own_pair.start()

    @pl.when(core == 0)
    def _():
        pltpu.make_async_copy(image_ref, rows_of(feats, 0), feat_recv.at[0]).start()
        pltpu.make_async_copy(image_head_ref, head.at[pl.ds(own_half, HALF)], head_recv.at[0]).start()

    @pl.when(core == 1)
    def _():
        pltpu.make_async_copy(text_ref, rows_of(feats, 0), feat_recv.at[0]).start()
        pltpu.make_async_copy(text_head_ref, head.at[pl.ds(own_half, HALF)], head_recv.at[0]).start()

    pl.semaphore_wait(barrier, 16 + leaves + turns)

    def half_rows(half, start, size):
        return pl.ds(pl.multiple_of(half * HALF + start, 16), size)

    def head_copy(src, n, start, size, device):
        return remote(src.at[pl.ds(pl.multiple_of(start, 16), size)], head.at[half_rows(f, start, size)],
                      head_send.at[n], head_recv.at[n + 1], device)

    def head_copies(src):
        return (
            head_copy(src, 1, DIRECT + SHARE * x, SHARE_FAR, far),
            head_copy(src, 2, DIRECT + SHARE * x + SHARE_FAR, SHARE_NEAR, near),
            head_copy(src, 0, 0, DIRECT, far),
        )

    def share_rows(owner, n):
        start = DIRECT + SHARE * owner + n * SHARE_FAR
        return half_rows(1 - f, start, (SHARE_FAR, SHARE_NEAR)[n])

    def share_copy(n, k):
        rows = share_rows(x, n)
        return remote(head.at[rows], head.at[rows], head_send.at[3 + 3 * n + k - 1],
                      head_recv.at[4 + 3 * n + k - 1], x_peers[k - 1])

    pair_copy = remote(pair_ref, pairs.at[1], pair_send.at[1], pair_recv, sibling)

    def bit_copy(src, src_slot, n, slot, device):
        start = slot * ROWS + n * BIT
        return remote(src.at[pl.ds(src_slot * ROWS + n * BIT, BIT)], feats.at[pl.ds(start, BIT)],
                      bit_send.at[slot // 4, n], bit_recv.at[slot - 2, n], device)

    def relay_in(src, n, device):
        rows = pl.ds(n * BIT, BIT)
        return remote(src.at[rows], relay.at[rows], bit_send.at[0, n], relay_recv.at[n], device)

    def relay_on(n, slot, device):
        return remote(relay.at[pl.ds(n * BIT, BIT)], feats.at[pl.ds(slot * ROWS + n * BIT, BIT)],
                      relay_send.at[n], bit_recv.at[slot - 2, n], device)

    def bit_wait(slot, n):
        bit_copy(feats, slot, n, slot, across).wait_recv()

    @pl.when(core == 0)
    def _():


        for copy in head_copies(image_head_ref):
            copy.start()

        @pl.when(leaves == 0)
        def _():
            for n in range(BITS):
                bit_copy(text_ref, 0, n, 3, shifted(index, 6)).start()

        @pl.when(leaves == 1)
        def _():
            for n in range(BITS):
                relay_in(text_ref, n, ahead).start()

        feat_copy(image_ref, step, 0, shifted(index, -step)).start()
        feat_copy(text_ref, 1, 1, sibling).start()

    @pl.when(core == 1)
    def _():

        for copy in head_copies(text_head_ref):
            copy.start()

        @pl.when(turns == 0)
        def _():
            for n in range(BITS):
                bit_copy(text_ref, 0, n, 2, shifted(index, 4)).start()

        @pl.when(turns == 1)
        def _():
            for n in range(BITS):
                relay_in(text_ref, n, across).start()

        feat_copy(image_ref, step, 0, shifted(index, -step)).start()
        feat_copy(image_ref, 2, 1, sibling).start()

    pair_copy.start()

    grad[...] = jnp.zeros_like(grad)

    @pl.when(core == 0)
    def _():
        rows_of(feats, 4)[...] = jnp.zeros((ROWS, E), jnp.bfloat16)
        rows_of(raw_grad, 4)[...] = jnp.zeros((ROWS, E), jnp.bfloat16)

    own_pair.wait()
    pair_copy.wait()
    signs[2] = jnp.ones((ROWS, ROWS), jnp.float32)
    for which in range(2):
        hit = lax.broadcasted_iota(jnp.int32, (ROWS, ROWS), 0) == pairs[which]
        sign = jnp.where(hit, -1.0, 1.0).astype(jnp.float32)

        @pl.when(core == 0)
        def _():
            signs[which] = sign.T

        @pl.when(core == 1)
        def _():
            signs[1 - which] = sign

    def feat_wait(slot):
        pltpu.make_async_copy(rows_of(feats, slot), rows_of(feats, slot), feat_recv.at[slot]).wait()

    def turn(slot):
        feats_t[:, slot * ROWS : (slot + 1) * ROWS] = rows_of(feats, slot)[...].T

    def head_wait(rows, sem):
        pltpu.make_async_copy(head.at[rows], head.at[rows], head_recv.at[sem]).wait()

    other_half = pl.multiple_of((1 - f) * HALF, 16)

    for n in range(2):
        head_wait(share_rows(x, n), 2 + n)
        for k in range(1, 4):
            share_copy(n, k).start()

    for n in range(BITS):
        @pl.when(leaves == 1)
        def _():
            relay_in(text_ref, n, ahead).wait_recv()
            relay_on(n, 3, device_of(x, yh, f, 0, 1)).start()

        @pl.when(turns == 1)
        def _():
            relay_in(text_ref, n, across).wait_recv()
            relay_on(n, 2, device_of(0, yh, f, 0, 1)).start()

        @pl.when(core == 1)
        def _():
            bit_wait(2, n)
            bit_copy(feats, 2, n, 4, shifted(index, 4)).start()

    @pl.when(core == 0)
    def _():
        feat_wait(2)

    for slot in (0, 1):
        feat_wait(slot)

    head_wait(pl.ds(own_half, HALF), 0)
    early = pl.ds(pl.multiple_of(f * (E - EARLY), 128), EARLY)
    late = pl.ds(pl.multiple_of((1 - f) * EARLY, 128), E - EARLY)

    def begin(slot, carry):
        rows_of(raw, slot)[...] = jnp.dot(
            rows_of(feats, slot)[:, early], head[early, :], preferred_element_type=jnp.float32
        )
        return carry

    lax.fori_loop(0, 3, begin, 0)
    for slot in (0, 1, 2):
        turn(slot)

    head_wait(half_rows(1 - f, 0, DIRECT), 1)
    for n in range(2):
        for k in range(1, 4):
            head_wait(share_rows(lax.rem(x + 4 - k, 4), n), 4 + 3 * n + k - 1)

    def emb_copy(slot):
        return remote(rows_of(emb, slot), rows_of(emb_other, slot),
                      emb_send.at[slot], emb_recv.at[slot], sibling)

    def embed(slot):
        product = rows_of(raw, slot)[...] + jnp.dot(
            rows_of(feats, slot)[:, late], head[late, :], preferred_element_type=jnp.float32
        )
        inverse = lax.rsqrt(jnp.sum(product * product, axis=1, keepdims=True) + 1e-06)
        unit = product * inverse
        rows_of(raw, slot)[...] = unit
        rows_of(inv, slot)[...] = inverse
        rows_of(emb, slot)[...] = unit.astype(jnp.bfloat16)
        emb_copy(slot).start()

    def embed_step(slot, carry):
        @pl.when((slot == 3) & (core == 0))
        def _():
            feat_wait(3)

        @pl.when((slot == 3) & (core == 1))
        def _():
            for n in range(BITS):
                bit_wait(3, n)

        @pl.when(slot == 3)
        def _():
            begin(3, 0)

        embed(slot)
        return carry

    lax.fori_loop(0, 4, embed_step, 0)

    @pl.when(core == 1)
    def _():
        for n in range(BITS):
            bit_wait(4, n)
        begin(4, 0)
        embed(4)

    turn(3)
    turn(4)

    for slot in range(4):
        @pl.when(core == 0)
        def _():
            emb_copy(slot).wait_recv()

        @pl.when(core == 1)
        def _():
            emb_copy(slot).wait_recv()

    @pl.when(core == 0)
    def _():
        emb_copy(4).wait_recv()

    scale = scale_ref[0]
    bias = bias_ref[0]

    def item(n, carry):
        at0 = lax.div(n, 2)
        at1 = lax.div(n + 1, 2)
        col0 = 1 - lax.div(at0, 2) + 2 * lax.rem(n, 2)
        col1 = 2 * lax.rem(n + 1, 2)
        at = at0 + core * (at1 - at0)
        col = col0 + core * (col1 - col0)
        kind = 2 - (
            is_equal(n, 0) * (2 - core) + is_equal(n, 4) * (1 - core) + is_equal(n, 1) * 2 * core
        )
        block = emb_other[pl.ds(pl.multiple_of(col * ROWS, ROWS), 2 * ROWS)]
        scores = scale * lax.dot_general(
            rows_of(emb, at)[...], block, (((1,), (1,)), ((), ())),
            preferred_element_type=jnp.float32,
        ) + bias
        sign = signs[kind]
        first = sign * (0.0625 + 0.0625 * jnp.tanh((0.5 * sign) * scores[:, :ROWS]))
        second = 0.0625 + 0.0625 * jnp.tanh(0.5 * scores[:, ROWS:])
        slope = jnp.concatenate([first, second], axis=1).astype(jnp.bfloat16)
        here = rows_of(grad, at)
        here[...] += jnp.dot(slope, block, preferred_element_type=jnp.float32)
        return carry

    lax.fori_loop(0, 8, item, 0)

    def finish(slot, carry):
        unit = rows_of(raw, slot)[...]
        slope = scale * rows_of(grad, slot)[...]
        inner = jnp.sum(unit * slope, axis=1, keepdims=True)
        rows_of(raw_grad, slot)[...] = (
            (slope - unit * inner) * rows_of(inv, slot)[...]
        ).astype(jnp.bfloat16)
        return carry

    lax.fori_loop(0, 4, finish, 0)

    @pl.when(core == 1)
    def _():
        finish(4, 0)

    SIDE = HALF // 2

    def cols_of(j):
        return pl.ds(STARTS[j], WIDTHS[j])

    def wide_of(j):
        return pl.ds(STARTS[j] + 128 * j, WIDTHS[j] + 128)

    def main_of(j):
        return pl.ds(STARTS[j] + 128 * j, WIDTHS[j])

    def rest_of(j):
        return pl.ds(STARTS[j] + 128 * j + WIDTHS[j], 128)

    def y_copies(j):
        cols = cols_of(j)
        return (
            remote(y_out.at[pl.ds(0, SIDE), cols], y_in.at[pl.ds(0, SIDE), cols],
                   y_send.at[j, 0], y_recv.at[j, 0], near),
            remote(y_out.at[pl.ds(SIDE, SIDE), cols], y_in.at[pl.ds(SIDE, SIDE), cols],
                   y_send.at[j, 1], y_recv.at[j, 1], far),
        )

    for j in range(PARTS):
        cols = cols_of(j)
        y_out[:, cols] = jnp.dot(
            feats_t[pl.ds(other_half, HALF), :], raw_grad[:, cols], preferred_element_type=jnp.float32
        ).astype(jnp.bfloat16)
        for copy in y_copies(j):
            copy.start()
    for j in range(PARTS):
        cols = cols_of(j)
        total[:, cols] = jnp.dot(
            feats_t[pl.ds(own_half, HALF), :], raw_grad[:, cols], preferred_element_type=jnp.float32
        )

    def x_copy(j, k):
        cols = cols_of(j)
        return remote(x_out.at[k - 1, :, cols], x_in.at[k - 1, :, cols],
                      x_send.at[j, k - 1], x_recv.at[j, k - 1], x_peers[k - 1])

    def z_copy(j, k):
        cols = wide_of(j)
        return remote(z_out.at[k - 1, :, cols], z_in.at[k - 1, :, cols],
                      z_send.at[j, k - 1], z_recv.at[j, k - 1], z_peers[k - 1])

    def y2_copy(j):
        cols = wide_of(j)
        return remote(z_sum.at[:, cols], y2_in.at[:, cols], y2_send.at[j], y2_recv.at[j], across)

    def zag_copy(j, k):
        cols = wide_of(j)
        return remote(final.at[:, cols], z_all.at[k - 1, :, cols],
                      zag_send.at[j, k - 1], zag_recv.at[j, k - 1], z_peers[k - 1])

    def x_rows(at):
        return pl.ds(pl.multiple_of(at * XROWS, 16), XROWS)

    def xag_copy(j, k, at):
        rows, cols = x_rows(at), cols_of(j)
        return remote(mine.at[rows, cols], mine.at[rows, cols],
                      xag_send.at[j, k - 1], xag_recv.at[j, k - 1], x_peers[k - 1])

    def core_copy(j):
        cols = cols_of(j)
        return remote(mine.at[:, cols], other.at[:, cols], core_send.at[j], core_recv.at[j], sibling)

    def stage_a(j):
        cols = cols_of(j)
        for copy in y_copies(j):
            copy.wait_recv()
        for k in range(1, 4):
            rows = x_rows(lax.rem(x + k, 4))
            x_out[k - 1, :, cols] = (
                total[rows, cols] + y_in[rows, cols].astype(jnp.float32)
            ).astype(jnp.bfloat16)
            x_copy(j, k).start()
        x_sum[:, cols] = total[x_rows(x), cols] + y_in[x_rows(x), cols].astype(jnp.float32)

    def extra_cols(j, at):
        block = lax.div(at * (WIDTHS[j] // 128), 8)
        return pl.ds(pl.multiple_of(STARTS[j] + block * 128, 128), 128)

    def piece_rows(at):
        return pl.ds(pl.multiple_of(at * PIECE, PIECE), PIECE)

    def stage_b(j):
        cols = cols_of(j)
        for k in range(1, 4):
            x_copy(j, k).wait_recv()
        x_sum[:, cols] = (
            x_sum[:, cols] + x_in[0, :, cols].astype(jnp.float32)
        ) + (x_in[1, :, cols].astype(jnp.float32) + x_in[2, :, cols].astype(jnp.float32))
        for k in range(1, 8):
            at = lax.rem(z + k, 8)
            z_out[k - 1, :, main_of(j)] = x_sum[piece_rows(at), cols].astype(jnp.bfloat16)
            z_out[k - 1, :, rest_of(j)] = x_sum[8 * PIECE :, extra_cols(j, at)].astype(jnp.bfloat16)
            z_copy(j, k).start()
        z_sum[:, main_of(j)] = x_sum[piece_rows(z), cols]
        z_sum[:, rest_of(j)] = x_sum[8 * PIECE :, extra_cols(j, z)]

    def stage_c(j):
        cols = wide_of(j)
        for k in range(1, 8):
            z_copy(j, k).wait_recv()
        acc = z_sum[:, cols]
        for k in range(1, 8):
            acc = acc + z_in[k - 1, :, cols].astype(jnp.float32)
        z_sum[:, cols] = acc
        y2_copy(j).start()

    def place(j, at, piece):
        rows = pl.ds(pl.multiple_of(x * XROWS + at * PIECE, PIECE), PIECE)
        mine[rows, cols_of(j)] = piece[:, : WIDTHS[j]]
        tail = pl.ds(pl.multiple_of(x * XROWS + 8 * PIECE, PIECE), PIECE)
        blocks = WIDTHS[j] // 128
        for n in range(blocks):
            @pl.when(at == -(-8 * n // blocks))
            def _():
                mine[tail, pl.ds(STARTS[j] + n * 128, 128)] = piece[:, WIDTHS[j] :]

    def stage_d(j):
        cols = wide_of(j)
        y2_copy(j).wait_recv()
        final[:, cols] = (z_sum[:, cols] + y2_in[:, cols]).astype(jnp.bfloat16)
        for k in range(1, 8):
            zag_copy(j, k).start()
        place(j, z, final[:, cols])

    def stage_e(j):
        for k in range(1, 8):
            zag_copy(j, k).wait_recv()
            place(j, lax.rem(z + 8 - k, 8), z_all[k - 1, :, wide_of(j)])
        for k in range(1, 4):
            xag_copy(j, k, x).start()

    def stage_f(j):
        for k in range(1, 4):
            xag_copy(j, k, lax.rem(x + 4 - k, 4)).wait_recv()
        core_copy(j).start()

    def out_copies(j, first, second):
        cols = cols_of(j)
        return (
            pltpu.make_async_copy(mine.at[:, cols], first.at[:, cols], out_sem.at[j, 0]),
            pltpu.make_async_copy(other.at[:, cols], second.at[:, cols], out_sem.at[j, 1]),
        )

    def stage_g(j):
        core_copy(j).wait_recv()

        @pl.when(core == 0)
        def _():
            for copy in out_copies(j, image_out, text_out):
                copy.start()

        @pl.when(core == 1)
        def _():
            for copy in out_copies(j, text_out, image_out):
                copy.start()

    stages = (stage_a, stage_b, stage_c, stage_d, stage_e, stage_f, stage_g)
    for turn_at in range(len(stages) + PARTS - 1):
        for j in range(PARTS):
            if 0 <= turn_at - j < len(stages):
                stages[turn_at - j](j)

    for copy in head_copies(image_head_ref):
        copy.wait_send()
    for n in range(2):
        for k in range(1, 4):
            share_copy(n, k).wait_send()

    for which in range(2):
        feat_copy(image_ref, 0, which, sibling).wait_send()
    for n in range(BITS):
        bit_copy(text_ref, 0, n, 2, across).wait_send()

    @pl.when(core == 1)
    def _():
        for n in range(BITS):
            bit_copy(feats, 2, n, 4, across).wait_send()
        emb_copy(4).wait_send()

    @pl.when(leaves + turns == 1)
    def _():
        for n in range(BITS):
            relay_on(n, 2, across).wait_send()

    for slot in range(4):
        emb_copy(slot).wait_send()
    for j in range(PARTS):
        for copy in y_copies(j):
            copy.wait_send()
        for k in range(1, 4):
            x_copy(j, k).wait_send()
            xag_copy(j, k, x).wait_send()
        for k in range(1, 8):
            z_copy(j, k).wait_send()
            zag_copy(j, k).wait_send()
        y2_copy(j).wait_send()
        core_copy(j).wait_send()
        for copy in out_copies(j, image_out, text_out):
            copy.wait()


def widen(image_ref, text_ref, image_out, text_out):
    image_out[...] = image_ref[...].astype(jnp.float32)
    text_out[...] = text_ref[...].astype(jnp.float32)


def on_device(
    image_features, text_features, image_head, text_head, pair_index, logit_scale, logit_bias
):
    hbm = pl.BlockSpec(memory_space=pl.ANY)
    smem = pl.BlockSpec(memory_space=pltpu.SMEM)
    bf16, f32 = jnp.bfloat16, jnp.float32
    vmem = pltpu.VMEM
    dma = pltpu.SemaphoreType.DMA
    image_half, text_half = pl.pallas_call(
        kernel,
        out_shape=(
            jax.ShapeDtypeStruct((HALF, E), bf16),
            jax.ShapeDtypeStruct((HALF, E), bf16),
        ),
        in_specs=[hbm, hbm, hbm, hbm, hbm, smem, smem],
        out_specs=(hbm, hbm),
        scratch_shapes=[
            vmem((SLOTS * ROWS, E), bf16),
            vmem((E, SLOTS * ROWS), bf16),
            vmem((E, E), bf16),
            vmem((SLOTS * ROWS, E), f32),
            vmem((SLOTS * ROWS, 1), f32),
            vmem((SLOTS * ROWS, E), bf16),
            vmem((SLOTS * ROWS, E), bf16),
            vmem((SLOTS * ROWS, E), f32),
            vmem((SLOTS * ROWS, E), bf16),
            vmem((ROWS, E), bf16),
            vmem((2, 1, ROWS), jnp.int32),
            vmem((3, ROWS, ROWS), f32),
            vmem((HALF, E), bf16),
            vmem((HALF, E), bf16),
            vmem((HALF, E), f32),
            vmem((3, XROWS, E), bf16),
            vmem((3, XROWS, E), bf16),
            vmem((XROWS, E), f32),
            vmem((7, PIECE, PWIDE), bf16),
            vmem((7, PIECE, PWIDE), bf16),
            vmem((PIECE, PWIDE), f32),
            vmem((PIECE, PWIDE), f32),
            vmem((PIECE, PWIDE), bf16),
            vmem((7, PIECE, PWIDE), bf16),
            vmem((HALF, E), bf16),
            vmem((HALF, E), bf16),
            dma((2,)),
            dma((SLOTS,)),
            dma((2, BITS)),
            dma((3, BITS)),
            dma((BITS,)),
            dma((BITS,)),
            dma((9,)),
            dma((10,)),
            dma((2,)),
            dma,
            dma((SLOTS,)),
            dma((SLOTS,)),
            dma((PARTS, 2)),
            dma((PARTS, 2)),
            dma((PARTS, 3)),
            dma((PARTS, 3)),
            dma((PARTS, 7)),
            dma((PARTS, 7)),
            dma((PARTS,)),
            dma((PARTS,)),
            dma((PARTS, 7)),
            dma((PARTS, 7)),
            dma((PARTS, 3)),
            dma((PARTS, 3)),
            dma((PARTS,)),
            dma((PARTS,)),
            dma((PARTS, 2)),
        ],
        compiler_params=pltpu.CompilerParams(
            collective_id=0, has_side_effects=True, vmem_limit_bytes=60 * 2**20
        ),
        cost_estimate=pl.CostEstimate(
            flops=12 * 10**9, bytes_accessed=12 * 10**6, transcendentals=10**6
        ),
    )(image_features, text_features, image_head, text_head, pair_index, logit_scale, logit_bias)
    block = pl.BlockSpec((HALF // WIDEN, E), lambda n: (n, 0))
    return pl.pallas_call(
        widen,
        grid=(WIDEN,),
        out_shape=(
            jax.ShapeDtypeStruct((HALF, E), f32),
            jax.ShapeDtypeStruct((HALF, E), f32),
        ),
        in_specs=[block, block],
        out_specs=(block, block),
        compiler_params=pltpu.CompilerParams(vmem_limit_bytes=60 * 2**20),
        cost_estimate=pl.CostEstimate(flops=2 * HALF * E, bytes_accessed=12 * HALF * E, transcendentals=0),
    )(image_half, text_half)


def solution(mesh):
    placed = (
        P(("blk", "fsdp"), None),
        P(("blk", "fsdp"), None),
        P("fsdp", None),
        P("fsdp", None),
        P(("blk", "fsdp"), None),
        P(),
        P(),
    )
    return jax.shard_map(
        on_device,
        mesh=mesh,
        in_specs=placed,
        out_specs=(P("fsdp", None), P("fsdp", None)),
        check_vma=False,
    )
```
